256 devices in a mesh: sub: 32 (over z, x), pf: 8 (over y, core).
Axes of the slice: x: 4, y: 4, z: 8, core: 2. Of those that a mesh axis runs over, the one named last changes fastest.
Arguments:
- visibilities: bfloat16 [8, 64, 65536], P(None, 'pf', 'sub'), may hold values from -0.125 to 0.125
- row_positions: bfloat16 [2, 65536], P(None, 'sub'), may hold values from -24 to 24
- channel_ratio: float32 [64], replicated, may hold values from 0.75 to 1.25
- row_subgrid: int32 [65536, 1], P('sub'), may hold values from 0 to 2047; in each aligned block of 2048 rows (0 to 2047, 2048 to 4095, ...) at most 2 rows name the same one
- row_count: int32 [32], P('sub'), may hold values from 1 to 2048, 52428 in all
- beam_terms: bfloat16 [2048, 2, 8, 4096], P(('sub', 'pf')), may hold values from -4 to 4
- subgrid_tile: int32 [2048, 1], P(('sub', 'pf')), may hold values from 0 to 31; in each aligned block of 8 rows (0 to 7, 8 to 15, ...) at most 2 rows name the same one
- offset_rows: int32 [2048], P(('sub', 'pf')), may hold values from 0 to 32
- offset_cols: int32 [2048], P(('sub', 'pf')), may hold values from 0 to 1984
Outputs:
- grid_band: float32 [256, 8, 96, 2048], P(('sub', 'pf'))
The draws below stay inside these ranges and needn't reach their ends.
Inputs may be any that keep to these rules, and one draw needn't show every extreme that they name: `row_subgrid`: among the 2048 rows of one index of sub, counted or not, no subgrid is named more than 2 times, a bound that some block reaches. `row_count`: rows at or beyond this count in their block are ignored; some block is full. `subgrid_tile`: subgrid g goes to the tile at this sub index and at the pf index of the device that holds g. Among the 8 subgrids of one device no value occurs more than 2 times, a bound that some device reaches.
All inputs are finite; a program needn't handle non-finite values.
Results may differ from the reference program's by a relative error of at most 0.0046.
Values may be sent and summed in bfloat16 or wider, within the bound.
No kernel may reach another device: no remote copies, remote signals or barrier semaphores. Data moves between devices by JAX's collectives and lax.ppermute only.
A program may use at most 128 MiB of HBM per device.

```python
import math
import jax
import jax.numpy as jnp
import numpy as np
from jax import lax

SUBPIX = 64
TILE = 2048
BAND = 96
SG_DEV = 8
R_DEV = 2048
CHAN = 64
ROWS = 65536
SUBGRIDS = 2048
TILES = 256
MOSTR = 2
CAPT = 2
N_SUB = 32
N_PF = 8


def plant(entries, rng, least, largest):
    place = [jax.random.randint(jax.random.fold_in(rng, axis), (), 0, length) for axis, length in enumerate(entries.shape)]
    main_axis = entries.shape.index(max(entries.shape))
    neighbour = place[:main_axis] + [(place[main_axis] + 1) % entries.shape[main_axis]] + place[main_axis + 1:]
    return entries.at[tuple(place)].set(least).at[tuple(neighbour)].set(largest)


def level_of(stream_key, dims, cuts, low, high):
    loudness, own = 1.0, jax.random.fold_in(stream_key, 6)
    for dim, parts in cuts:
        draws = jnp.exp(jax.random.uniform(jax.random.fold_in(own, dim), (parts,), jnp.float32, low / len(cuts), high / len(cuts)))
        loudness = loudness * jnp.repeat(draws, dims[dim] // parts).reshape([-1 if axis == dim else 1 for axis in range(len(dims))])
    return loudness


def split_up(number_of, total, limit, lean):
    weights = [(1 << 20) // math.isqrt(rank ** lean) + 1 for rank in range(2, number_of + 1)]
    surplus, given = total - limit - (number_of - 1), [1] * (number_of - 1)
    while surplus > 0:
        free = [i for i in range(number_of - 1) if given[i] < limit]
        mass, budget = sum([weights[i] for i in free]), surplus
        for i in free:
            extra = min(limit - given[i], max(1, budget * weights[i] // mass), surplus)
            given[i] = given[i] + extra
            surplus = surplus - extra
    return np.array([limit] + given)


def uneven_parts(rng, number_of, total, limit, slope):
    if number_of == 2:
        one = jax.random.randint(rng, (), max(1, total - limit), min(limit, total - 1) + 1)
        return jnp.stack([one, total - one])
    sizes = jnp.asarray(split_up(number_of, total, limit, slope), jnp.int32)
    twos = (number_of - 1) // 2
    donor, taker = sizes[1:1 + 2 * twos:2], sizes[2:2 + 2 * twos:2]
    room = jnp.minimum(donor - 1, limit - taker)
    moved = jax.random.randint(jax.random.fold_in(rng, 1), (twos,), 0, 1 << 20) % (room + 1)
    sizes = sizes.at[1:1 + 2 * twos:2].set(donor - moved).at[2:2 + 2 * twos:2].set(taker + moved)
    return sizes[jax.random.permutation(jax.random.fold_in(rng, 2), number_of)]


def deal_out(rng, own, number, rows, number_of, top, most, slope):
    order = jax.random.permutation(rng, number_of)
    packed, common = shares(number_of, rows * top, most, slope, True), shares(number_of, rows * top, most, slope, False)
    places = jnp.arange(number_of)

    def named(tallies, rotation):
        used = int((tallies > 0).sum())
        fixed = max(1, used // 4)
        passed = fixed + (places - fixed + rotation * (used - fixed)) % max(1, number_of - fixed)
        return jnp.zeros((number_of,), jnp.int32).at[order[jnp.where(places < fixed, places, passed)]].set(jnp.asarray(tallies, jnp.int32))

    tallies = jnp.where(number % 4 == 0, named(packed, number // 4), named(common, number - number // 4 - 1))
    mixed = jax.random.permutation(jax.random.fold_in(own, 3), number_of)
    donor, receiver = mixed[0:number_of // 2 * 2:2], mixed[1:number_of // 2 * 2:2]
    slack = jnp.minimum(tallies[donor] - 1, most - tallies[receiver]) // 2
    slack = jnp.where((donor == order[0]) | (receiver == order[0]) | (tallies[receiver] == 0), 0, jnp.maximum(slack, 0))
    passed = jax.random.randint(jax.random.fold_in(own, 4), (number_of // 2,), 0, 1 << 20) % (slack + 1)
    tallies = tallies.at[donor].add(-passed).at[receiver].add(passed)
    items = jnp.searchsorted(jnp.cumsum(tallies), jnp.arange(rows * top), side="right").astype(jnp.int32)
    table = items.reshape(top, rows).T
    table = table[jax.random.permutation(jax.random.fold_in(own, 1), rows)]
    rotation = jax.random.randint(jax.random.fold_in(own, 2), (rows, 1), 0, top)
    return jnp.take_along_axis(table, (jnp.arange(top)[None, :] + rotation) % top, axis=1)


def shares(amount, total, bound, lean, full):
    weights = [(1 << 20) // math.isqrt(standing ** lean) + 1 for standing in range(1, amount + 1)]
    largest = bound if full else min(bound, max(-(-total // amount), total * weights[0] // sum(weights)))
    least = 1 if total - largest >= amount - 1 else 0
    holding, surplus = [largest] + [least] * (amount - 1), total - largest - least * (amount - 1)
    while surplus > 0:
        movable = [i for i in range(1, amount) if holding[i] < largest] or [i for i in range(1, amount) if holding[i] < bound]
        mass, remaining = sum([weights[i] for i in movable]), surplus
        for i in movable:
            extra = min(bound - holding[i], max(1, remaining * weights[i] // mass), surplus)
            holding[i] = holding[i] + extra
            surplus = surplus - extra
    return np.array(holding)


def noise(key, dims, scale, limit, split=(), held_as=jnp.bfloat16):
    level = level_of(key, dims, split, -0.22, 0.18) if split else 1.0
    values = jax.random.normal(key, dims, jnp.float32) * scale * level
    return jnp.minimum(jnp.maximum(values, -limit), limit).astype(held_as)


def setup_inputs(seed: int = 0) -> dict:
    splits = jax.random.split(jax.random.key(seed), 10)
    visibilities = noise(splits[0], (8, CHAN, ROWS), ((SUBGRIDS / (R_DEV * N_SUB * CHAN)) ** 0.5), 0.125, ((1, 8), (2, 32)))
    row_positions = jnp.clip(jax.random.uniform(splits[1], (2, ROWS), jnp.float32, -24.0, 24.0) * level_of(splits[1], (2, ROWS), ((1, 32),), -0.4, 0.0), -24.0, 24.0).astype(jnp.bfloat16)
    channel_ratio = jnp.clip(jax.random.uniform(splits[2], (CHAN,), jnp.float32, 0.75, 1.25), 0.75, 1.25)
    row_subgrid_keys = jax.random.split(jax.random.fold_in(splits[3], 1), ROWS // R_DEV)
    row_subgrid_turns = jax.random.permutation(jax.random.fold_in(splits[3], 3), ROWS // R_DEV)
    row_subgrid = jax.vmap(lambda own, number: deal_out(jax.random.fold_in(splits[3], 2), own, number, R_DEV, SUBGRIDS, 1, MOSTR, 1))(row_subgrid_keys, row_subgrid_turns).reshape((ROWS, 1))
    row_count = uneven_parts(splits[4], N_SUB, (4 * R_DEV * N_SUB) // 5, R_DEV, 2).astype(jnp.int32)
    beam_terms = noise(splits[5], (SUBGRIDS, 2, 8, SUBPIX * SUBPIX), 0.7, 4.0, ((0, 256),))
    subgrid_tile_keys = jax.random.split(jax.random.fold_in(splits[6], 1), SUBGRIDS // SG_DEV)
    subgrid_tile_turns = jax.random.permutation(jax.random.fold_in(splits[6], 3), SUBGRIDS // SG_DEV)
    subgrid_tile = jax.vmap(lambda own, number: deal_out(jax.random.fold_in(splits[6], 2), own, number, SG_DEV, N_SUB, 1, CAPT, 2))(subgrid_tile_keys, subgrid_tile_turns).reshape((SUBGRIDS, 1))
    offset_rows = plant(jax.random.randint(splits[7], (SUBGRIDS,), 0, BAND - SUBPIX + 1), jax.random.fold_in(splits[7], 1), 0, BAND - SUBPIX).astype(jnp.int32)
    offset_cols = plant(jax.random.randint(splits[8], (SUBGRIDS,), 0, TILE - SUBPIX + 1), jax.random.fold_in(splits[8], 1), 0, TILE - SUBPIX).astype(jnp.int32)
    return dict(visibilities=visibilities, row_positions=row_positions, channel_ratio=channel_ratio, row_subgrid=row_subgrid, row_count=row_count, beam_terms=beam_terms, subgrid_tile=subgrid_tile, offset_rows=offset_rows, offset_cols=offset_cols)


two_pi = 2.0 * math.pi


def row_slots(subgrid_ids, row_limit, slot_groups, slot_depth):
    length = subgrid_ids.shape[0]
    positions = jnp.arange(length, dtype=jnp.int32)
    counted = positions < row_limit
    sort_key = jnp.where(counted, subgrid_ids, slot_groups).astype(jnp.int32)
    ordering = jnp.argsort(sort_key, stable=True).astype(jnp.int32)
    sorted_keys = sort_key[ordering]
    first_seen = jnp.searchsorted(sorted_keys, sorted_keys, side="left").astype(jnp.int32)
    rank_within = jnp.zeros((length,), jnp.int32).at[ordering].set(positions - first_seen)
    return jnp.where(counted, subgrid_ids * slot_depth + rank_within, slot_groups * slot_depth).astype(jnp.int32)


def pixel_axis(pixels):
    return (jnp.arange(pixels, dtype=jnp.float32) - pixels // 2) / pixels


def subgrid_image(samples, positions, ratios, pixels):
    scaled = positions.astype(jnp.float32)[:, :, None, :] * ratios[None, None, :, None]
    along_u = scaled[:, 0].reshape(-1)
    along_v = scaled[:, 1].reshape(-1)
    values = jnp.moveaxis(samples, 2, 0).reshape(8, -1).astype(jnp.float32)
    coords_x = pixel_axis(pixels)
    phase_u = two_pi * along_u[:, None] * coords_x[None, :]
    phase_v = two_pi * along_v[:, None] * coords_x[None, :]
    cos_u = jnp.cos(phase_u)
    sin_u = jnp.sin(phase_u)
    real_part = values[0::2][:, :, None]
    imag_part = values[1::2][:, :, None]
    left_re = real_part * cos_u[None] - imag_part * sin_u[None]
    left_im = real_part * sin_u[None] + imag_part * cos_u[None]
    stacked = jnp.concatenate([left_re, left_im], 0)
    weighted = jnp.transpose(stacked, (1, 0, 2)).reshape(stacked.shape[1], 8 * pixels).astype(jnp.bfloat16)
    phased = jnp.concatenate([jnp.cos(phase_v), jnp.sin(phase_v)], 1).astype(jnp.bfloat16)
    weighted = lax.optimization_barrier(weighted).astype(jnp.float32)
    phased = lax.optimization_barrier(phased).astype(jnp.float32)
    product = lax.dot_general(weighted, phased, (((0,), (0,)), ((), ())), precision=lax.Precision.HIGHEST, preferred_element_type=jnp.float32)
    product = product.reshape(2, 4, pixels, 2, pixels)
    image_re = product[0, :, :, 0] - product[1, :, :, 1]
    image_im = product[0, :, :, 1] + product[1, :, :, 0]
    return jnp.stack([image_re, image_im], 1).reshape(8, pixels, pixels)


def entry_of(matrix_parts, upper_index, lower_index):
    position = 2 * (2 * upper_index + lower_index)
    return matrix_parts[position], matrix_parts[position + 1]


def complex_times(first_term, second_term):
    return (first_term[0] * second_term[0] - first_term[1] * second_term[1],
            first_term[0] * second_term[1] + first_term[1] * second_term[0])


def conj_times(first_term, second_term):
    return (first_term[0] * second_term[0] + first_term[1] * second_term[1],
            first_term[0] * second_term[1] - first_term[1] * second_term[0])


def complex_plus(first_term, second_term):
    return first_term[0] + second_term[0], first_term[1] + second_term[1]


def taper_window(pixels):
    ramp = jnp.cos(two_pi * (jnp.arange(pixels, dtype=jnp.float32) + 0.5) / pixels)
    window = 0.55 - 0.45 * ramp
    return window[:, None] * window[None, :]


def apply_beams(image, beams, pixels):
    left_beam = beams[0].astype(jnp.float32).reshape(8, pixels, pixels)
    right_beam = beams[1].astype(jnp.float32).reshape(8, pixels, pixels)
    middle = {}
    for upper_index in range(2):
        for lower_index in range(2):
            middle[(upper_index, lower_index)] = complex_plus(
                conj_times(entry_of(left_beam, 0, upper_index), entry_of(image, 0, lower_index)),
                conj_times(entry_of(left_beam, 1, upper_index), entry_of(image, 1, lower_index)))
    window = taper_window(pixels)
    pieces = []
    for upper_index in range(2):
        for lower_index in range(2):
            result = complex_plus(
                complex_times(middle[(upper_index, 0)], entry_of(right_beam, 0, lower_index)),
                complex_times(middle[(upper_index, 1)], entry_of(right_beam, 1, lower_index)))
            pieces.append(result[0] * window)
            pieces.append(result[1] * window)
    return jnp.stack(pieces, 0)


def fourier_tables(pixels):
    centred = jnp.arange(pixels, dtype=jnp.int32) - pixels // 2
    product = (centred[:, None] * centred[None, :]) % pixels
    angle = -two_pi * product.astype(jnp.float32) / pixels
    return jnp.cos(angle), jnp.sin(angle)


def to_fourier(image, pixels):
    table_re, table_im = fourier_tables(pixels)
    image_re = image[0::2]
    image_im = image[1::2]
    highest = lax.Precision.HIGHEST

    def apply_left(matrix, operand):
        return jnp.einsum("al,qlm->qam", matrix, operand, precision=highest)

    def apply_right(operand, matrix):
        return jnp.einsum("qam,bm->qab", operand, matrix, precision=highest)

    mid_re = apply_left(table_re, image_re) - apply_left(table_im, image_im)
    mid_im = apply_left(table_re, image_im) + apply_left(table_im, image_re)
    out_re = apply_right(mid_re, table_re) - apply_right(mid_im, table_im)
    out_im = apply_right(mid_re, table_im) + apply_right(mid_im, table_re)
    return jnp.stack([out_re, out_im], 1).reshape(8, pixels, pixels) / pixels


def finish_subgrid(image, beams, pixels):
    return to_fourier(apply_beams(image, beams, pixels), pixels).astype(jnp.bfloat16)


def reference(visibilities, row_positions, channel_ratio, row_subgrid, row_count, beam_terms, subgrid_tile, offset_rows, offset_cols):
    slot_span = SUBGRIDS * MOSTR
    blocked_ids = row_subgrid[:, 0].reshape(N_SUB, R_DEV)
    slot_table = jax.vmap(lambda ids_block, limit_value: row_slots(ids_block, limit_value, SUBGRIDS, MOSTR))(blocked_ids, row_count)
    block_base = (jnp.arange(N_SUB, dtype=jnp.int32) * slot_span)[:, None]
    placed = jnp.where(slot_table < slot_span, slot_table + block_base, N_SUB * slot_span).reshape(-1).astype(jnp.int32)
    spread = jnp.zeros((8, CHAN, N_SUB * slot_span), jnp.bfloat16).at[:, :, placed].set(visibilities, mode="drop")
    spread = jnp.transpose(spread.reshape(8, CHAN, N_SUB, SUBGRIDS, MOSTR), (3, 2, 1, 0, 4))
    place_spread = jnp.zeros((2, N_SUB * slot_span), jnp.bfloat16).at[:, placed].set(row_positions, mode="drop")
    place_spread = jnp.transpose(place_spread.reshape(2, N_SUB, SUBGRIDS, MOSTR), (2, 1, 0, 3))

    def one_subgrid(operands):
        samples, positions, beams = operands
        image = subgrid_image(samples, positions, channel_ratio, SUBPIX)
        return finish_subgrid(image, beams, SUBPIX)

    fourier = lax.map(one_subgrid, (spread, place_spread, beam_terms))
    holder = jnp.arange(SUBGRIDS, dtype=jnp.int32) // SG_DEV
    target = (subgrid_tile[:, 0] * N_PF + holder % N_PF).astype(jnp.int32)
    grid_start = jnp.zeros((TILES, 8, BAND, TILE), jnp.float32)

    def deposit(subgrid_index, grid_now):
        patch_value = fourier[subgrid_index].astype(jnp.float32)
        corner = (target[subgrid_index], jnp.int32(0), offset_rows[subgrid_index], offset_cols[subgrid_index])
        current = lax.dynamic_slice(grid_now, corner, (1, 8, SUBPIX, SUBPIX))
        return lax.dynamic_update_slice(grid_now, current + patch_value[None], corner)

    return lax.fori_loop(0, SUBGRIDS, deposit, grid_start)
```

```python
import math

import jax
import jax.numpy as jnp
import numpy as np
from jax import lax
from jax.experimental import pallas as pl
from jax.experimental.pallas import tpu as pltpu
from jax.sharding import PartitionSpec as P

SUBPIX = 64
TILE = 2048
BAND = 96
N_SUB = 32
N_PF = 8
SG = 8
ROWS = 2048
F32 = jnp.float32
BF16 = jnp.bfloat16
MIB = 1 << 20
LIST = 72


def fit_even_odd():
    x = np.cos(np.pi * (np.arange(400) + 0.5) / 400) * 0.125 + 0.125
    r = np.sqrt(x)
    cheb = np.polynomial.chebyshev.Chebyshev
    out = []
    for values, degree in ((np.cos(2 * np.pi * r), 7), (np.sin(2 * np.pi * r) / r, 7)):
        poly = cheb.fit(x, values, degree, domain=[0.0, 0.25]).convert(kind=np.polynomial.Polynomial)
        out.append([float(c) for c in poly.coef])
    return out


COS_COEF, SIN_COEF = fit_even_odd()


def horner(coef, x):
    total = jnp.full_like(x, coef[-1])
    for c in coef[-2::-1]:
        total = total * x + c
    return total


def cos_sin_turns(t):
    r = t - jnp.round(t)
    r2 = r * r
    return horner(COS_COEF, r2), horner(SIN_COEF, r2) * r


def split_hi_lo(x):
    hi = x.astype(BF16)
    return hi, (x - hi.astype(F32)).astype(BF16)


def dft_tables():
    centred = np.arange(SUBPIX) - SUBPIX // 2
    angle = -2.0 * np.pi * ((centred[:, None] * centred[None, :]) % SUBPIX) / SUBPIX
    c, s = np.cos(angle), np.sin(angle)
    right = np.block([[c, s], [-s, c]])
    left = np.block([[c, -s], [s, c]]) / SUBPIX

    def parts(m):
        hi = m.astype(np.float32).astype(BF16)
        lo = (m - hi.astype(np.float64)).astype(np.float32).astype(BF16)
        return hi, lo

    rh, rl = parts(right)
    lh, ll = parts(left)
    ramp = np.cos(2 * np.pi * (np.arange(SUBPIX) + 0.5) / SUBPIX)
    window = 0.55 - 0.45 * ramp
    window = (window[:, None] * window[None, :]).astype(np.float32)
    return np.concatenate([rh, rh], 0), rl, np.concatenate([lh, lh], 1), ll, window


def exchange(tiles, lane, low_bit):
    tiles = list(tiles)
    for b in range(3):
        step = 1 << (low_bit + b)
        upper = ((lane >> (low_bit + b)) & 1) == 1
        for i in range(8):
            if (i >> b) & 1:
                continue
            k = i | (1 << b)
            first, second = tiles[i], tiles[k]
            tiles[i] = jnp.where(upper, pltpu.roll(second, step, 1), first)
            tiles[k] = jnp.where(upper, second, pltpu.roll(first, 128 - step, 1))
    return tiles


def dispatch_kernel(count_ref, data_ref, idcol_ref, idrow_ref, facts_ref, send_ref, slot_scr):
    count = count_ref[0]
    lane = lax.broadcasted_iota(jnp.int32, (128, 128), 1)
    row_in = lax.broadcasted_iota(jnp.int32, (128, 128), 0)
    for block in range(ROWS // 128):
        ids = jnp.broadcast_to(idcol_ref[block * 128 : (block + 1) * 128, :], (128, 128))

        def seen(chunk, hits):
            return jnp.where(ids == idrow_ref[pl.ds(chunk, 1), :], 1, hits)

        hits = lax.fori_loop(0, block, seen, jnp.zeros((128, 128), jnp.int32))
        here = (ids == idrow_ref[block : block + 1, :]) & (lane < row_in)
        hits = jnp.where(here, 1, hits)
        rank = jnp.max(hits, axis=1, keepdims=True)
        slot = jnp.where(row_in + block * 128 < count, ids * 2 + rank, -4096)
        slot_scr[block * 128 : (block + 1) * 128, :] = slot - lane

    data = data_ref[...]
    facts = facts_ref[...]
    tile_lane = lax.broadcasted_iota(jnp.int32, (8, 128), 1)

    def one_owner(owner, carry):
        rel = slot_scr[...]
        first = owner * 256
        picks = jnp.concatenate(
            [
                jnp.where(rel == first, 1.0, 0.0).astype(BF16),
                jnp.where(rel == first + 128, 1.0, 0.0).astype(BF16),
            ],
            1,
        )
        placed = jnp.dot(data, picks, preferred_element_type=F32)
        for half in range(2):
            part = placed[:, half * 128 : (half + 1) * 128]
            tiles = exchange([part[c * 8 : (c + 1) * 8] for c in range(8)], tile_lane, 4)
            tiles = tiles + [part[64:72] + facts[:8], facts[8:]]
            send_ref[owner * 2 + half] = jnp.concatenate(tiles, 0).astype(BF16)
        return carry

    lax.fori_loop(0, N_SUB // 2, one_owner, 0)


def dispatch(data, idcol, idrow, count, facts):
    vmem = pl.BlockSpec(memory_space=pltpu.VMEM)
    return pl.pallas_call(
        dispatch_kernel,
        out_shape=jax.ShapeDtypeStruct((N_SUB, 80, 128), BF16),
        in_specs=[pl.BlockSpec(memory_space=pltpu.SMEM)] + [vmem] * 4,
        out_specs=vmem,
        scratch_shapes=[pltpu.VMEM((ROWS, 128), jnp.int32)],
        compiler_params=pltpu.CompilerParams(vmem_limit_bytes=48 * MIB),
        name="dispatch",
    )(count, data, idcol, idrow, facts)


def cmul(a, b):
    return a[0] * b[0] - a[1] * b[1], a[0] * b[1] + a[1] * b[0]


def conj_mul(a, b):
    return a[0] * b[0] + a[1] * b[1], a[0] * b[1] - a[1] * b[0]


def cadd(a, b):
    return a[0] + b[0], a[1] + b[1]


def corrected_image(image, left, right, window):
    middle = {}
    for i in range(2):
        for j in range(2):
            middle[i, j] = cadd(conj_mul(left[i], image[j]), conj_mul(left[2 + i], image[2 + j]))
    out = []
    for i in range(2):
        for j in range(2):
            re, im = cadd(cmul(middle[i, 0], right[j]), cmul(middle[i, 1], right[2 + j]))
            out.append((re * window, im * window))
    return out


def phases(base_turns, tile_turns):
    cb, sb = cos_sin_turns(base_turns)
    ca, sa = cos_sin_turns(tile_turns)
    cos_out, sin_out = [], []
    for a in range(8):
        c, s = ca[a : a + 1], sa[a : a + 1]
        cos_out.append(cb * c - sb * s)
        sin_out.append(cb * s + sb * c)
    return jnp.concatenate(cos_out, 0), jnp.concatenate(sin_out, 0)


def subgrid_kernel(
    slot_ref, pf_ref, filled_ref, recv_ref, posu_ref, posv_ref, ratio_ref, beam_ref, rt2_ref, rtl_ref, lt2_ref, ltl_ref,
    window_ref, send_ref, vis_scr, u_scr, v_scr, list_scr, patch_scr, sems,
):
    tile_lane = lax.broadcasted_iota(jnp.int32, (8, 128), 1)

    odd = (tile_lane & 1) == 1

    def regroup(source, counts):
        tiles = exchange([recv_ref[p, source].astype(F32) for p in range(8)], tile_lane, 1)
        counts = list(counts)
        for g in range(SG):
            vis_scr[g * 64 + source * 2] = jnp.where(odd, pltpu.roll(tiles[g], 1, 1), tiles[g])
            vis_scr[g * 64 + source * 2 + 1] = jnp.where(odd, tiles[g], pltpu.roll(tiles[g], 127, 1))
            for j in range(2):
                list_scr[g * LIST + counts[g]] = g * 64 + source * 2 + j
                counts[g] = counts[g] + filled_ref[source * 16 + g * 2 + j]
        return tuple(counts)

    counts = lax.fori_loop(0, N_SUB, regroup, (jnp.int32(0),) * SG)
    for g in range(SG):
        for k in range(8):
            list_scr[g * LIST + counts[g] + k] = 512
        list_scr[SG * LIST + g] = counts[g]
    for scr in (vis_scr, u_scr, v_scr):
        scr[512] = jnp.zeros((8, 128), F32)

    sel_row = lax.broadcasted_iota(jnp.int32, (128, 128), 0)
    ratio = ratio_ref[...]
    base = pf_ref[0] * 16
    for j in range(2):
        for g in range(SG):
            pick = jnp.where(sel_row == base + (g * 2 + j), 1.0, 0.0).astype(BF16)
            for pos_ref, scr in ((posu_ref, u_scr), (posv_ref, v_scr)):
                scaled = jnp.dot(pos_ref[...], pick, preferred_element_type=F32) * ratio
                for s in range(N_SUB):
                    scr[g * 64 + s * 2 + j] = jnp.broadcast_to(scaled[s : s + 1], (8, 128))

    units = 4
    eight = lax.broadcasted_iota(jnp.int32, (8, 128 * units), 0).astype(F32)
    base_x = eight * (1.0 / 64.0)
    tile_x = (eight - 4.0) * (1.0 / 8.0)
    half_lane = lax.broadcasted_iota(jnp.int32, (SUBPIX, 128), 1) < SUBPIX
    window = window_ref[...]

    def one_subgrid(g, carry):
        def accumulate(step, total):
            first = g * LIST + step * (2 * units)
            picked = [list_scr[first + k] for k in range(2 * units)]

            def lanes(scr):
                return jnp.concatenate(
                    [
                        jnp.where(odd, scr[picked[2 * k + 1]], scr[picked[2 * k]])
                        for k in range(units)
                    ],
                    1,
                )

            u, v, vis = lanes(u_scr), lanes(v_scr), lanes(vis_scr)
            cos_u, sin_u = phases(u * base_x, u * tile_x)
            cos_v, sin_v = phases(v * base_x, v * tile_x)
            rows = []
            for q in range(4):
                re, im = vis[2 * q : 2 * q + 1], vis[2 * q + 1 : 2 * q + 2]
                rows.append((re * cos_u - im * sin_u).astype(BF16))
                rows.append((re * sin_u + im * cos_u).astype(BF16))
            left = jnp.concatenate(rows, 0)
            right = jnp.concatenate([cos_v.astype(BF16), sin_v.astype(BF16)], 0)
            return total + lax.dot_general(
                left, right, (((1,), (1,)), ((), ())), preferred_element_type=F32
            )

        steps = (list_scr[SG * LIST + g] + (2 * units - 1)) // (2 * units)
        total = lax.fori_loop(0, steps, accumulate, jnp.zeros((512, 128), F32))
        image = []
        for q in range(4):
            re = total[q * 128 : q * 128 + 64]
            im = total[q * 128 + 64 : q * 128 + 128]
            image.append((re[:, :64] - im[:, 64:], re[:, 64:] + im[:, :64]))
        beams = [
            [
                (beam_ref[g, side, 2 * e].astype(F32), beam_ref[g, side, 2 * e + 1].astype(F32))
                for e in range(4)
            ]
            for side in range(2)
        ]
        pieces = corrected_image(image, beams[0], beams[1], window)
        stacked = jnp.concatenate([jnp.concatenate([re, im], 1) for re, im in pieces], 0)
        hi, lo = split_hi_lo(stacked)
        mid = jnp.dot(jnp.concatenate([hi, lo], 1), rt2_ref[...], preferred_element_type=F32)
        mid = mid + jnp.dot(hi, rtl_ref[...], preferred_element_type=F32)
        mids = [mid[q * 64 : (q + 1) * 64] for q in range(4)]
        upper, lower = [], []
        for q in (0, 2):
            upper.append(jnp.where(half_lane, mids[q], pltpu.roll(mids[q + 1], 64, 1)))
            lower.append(jnp.where(half_lane, pltpu.roll(mids[q], 64, 1), mids[q + 1]))
        both = jnp.concatenate([jnp.concatenate(upper, 1), jnp.concatenate(lower, 1)], 0)
        hi, lo = split_hi_lo(both)
        out = jnp.dot(lt2_ref[...], jnp.concatenate([hi, lo], 0), preferred_element_type=F32)
        out = out + jnp.dot(ltl_ref[...], hi, preferred_element_type=F32)
        patch_scr[g] = out.astype(BF16)
        pltpu.make_async_copy(patch_scr.at[g], send_ref.at[slot_ref[g]], sems.at[g]).start()
        return carry

    lax.fori_loop(0, SG, one_subgrid, 0)

    def finish(g, carry):
        pltpu.make_async_copy(patch_scr.at[g], send_ref.at[slot_ref[g]], sems.at[g]).wait()
        return carry

    lax.fori_loop(0, SG, finish, 0)


def make_patches(slots, pf_index, filled, recv, pos_u, pos_v, ratio, beams, n_slots):
    vmem = pl.BlockSpec(memory_space=pltpu.VMEM)
    smem = pl.BlockSpec(memory_space=pltpu.SMEM)
    return pl.pallas_call(
        subgrid_kernel,
        out_shape=jax.ShapeDtypeStruct((n_slots, 128, 256), BF16),
        in_specs=[smem] * 3 + [vmem] * 10,
        out_specs=pl.BlockSpec(memory_space=pl.ANY),
        scratch_shapes=[
            pltpu.VMEM((SG * 64 + 1, 8, 128), F32),
            pltpu.VMEM((SG * 64 + 1, 8, 128), F32),
            pltpu.VMEM((SG * 64 + 1, 8, 128), F32),
            pltpu.SMEM((SG * LIST + SG,), jnp.int32),
            pltpu.VMEM((SG, 128, 256), BF16),
            pltpu.SemaphoreType.DMA((SG,)),
        ],
        compiler_params=pltpu.CompilerParams(vmem_limit_bytes=48 * MIB),
        name="subgrids",
    )(slots, pf_index, filled, recv, pos_u, pos_v, ratio, beams, *dft_tables())


def deposit_kernel(used_ref, row_ref, col_ref, recv_ref, out_ref):
    out_ref[...] = jnp.zeros_like(out_ref)
    tall = SUBPIX + 8
    lane = lax.broadcasted_iota(jnp.int32, (2 * tall, 256), 1)
    blank = jnp.zeros((8, 256), F32)

    def one_slot(slot, carry):
        @pl.when(used_ref[slot] > 0)
        def _():
            row, col = row_ref[slot], col_ref[slot]
            top = pl.multiple_of(jnp.minimum((row // 8) * 8, BAND - tall), 8)
            start = pl.multiple_of(jnp.minimum((col // 128) * 128, TILE - 256), 128)
            shift = col - start
            patch = recv_ref[slot].astype(F32)
            patch = jnp.concatenate([patch[:SUBPIX], blank, patch[SUBPIX:], blank], 0)
            patch = pltpu.roll(patch, row - top, 0)
            inside = (lane >= shift) & (lane < shift + SUBPIX)
            for q in range(4):
                moved = pltpu.roll(patch, lax.rem(shift + 256 - q * 64, 256), 1)
                moved = jnp.where(inside, moved, 0.0)
                for s in range(2):
                    spot = (0, 2 * q + s, pl.ds(top, tall), pl.ds(start, 256))
                    out_ref[spot] += moved[s * tall : (s + 1) * tall]

        return carry

    lax.fori_loop(0, used_ref.shape[0], one_slot, 0)


def deposit(used, rows, cols, recv):
    vmem = pl.BlockSpec(memory_space=pltpu.VMEM)
    smem = pl.BlockSpec(memory_space=pltpu.SMEM)
    return pl.pallas_call(
        deposit_kernel,
        out_shape=jax.ShapeDtypeStruct((1, 8, BAND, TILE), F32),
        in_specs=[smem, smem, smem, vmem],
        out_specs=vmem,
        compiler_params=pltpu.CompilerParams(vmem_limit_bytes=48 * MIB),
        name="deposit",
    )(used, rows, cols, recv)


def shards(
    visibilities,
    row_positions,
    channel_ratio,
    row_subgrid,
    row_count,
    beam_terms,
    subgrid_tile,
    offset_rows,
    offset_cols,
):
    me_sub = lax.axis_index("sub")
    me_pf = lax.axis_index("pf")
    tile_of = subgrid_tile[:, 0]
    earlier = jnp.arange(SG)[:, None] > jnp.arange(SG)[None, :]
    rank = jnp.sum((tile_of[:, None] == tile_of[None, :]) & earlier, 1).astype(jnp.int32)
    slots = tile_of * 2 + rank
    facts = jnp.stack([slots, offset_rows, offset_cols // 128, offset_cols % 128], 0)
    facts = jnp.pad(facts.astype(F32), ((3, 9), (0, 120)))
    data = jnp.concatenate(
        [
            jnp.transpose(visibilities, (1, 0, 2)).reshape(64, ROWS),
            row_positions,
            jnp.ones((1, ROWS), BF16),
            jnp.zeros((13, ROWS), BF16),
        ],
        0,
    )
    send = dispatch(data, row_subgrid, row_subgrid.reshape(ROWS // 128, 128), row_count, facts)
    recv = lax.all_to_all(send, "sub", split_axis=0, concat_axis=0, tiled=True)
    notes = recv[:, 64:80]
    recv = jnp.transpose(recv[:, :64].reshape(N_SUB, N_PF, 8, 128), (1, 0, 2, 3))
    recv = lax.all_to_all(recv, "pf", split_axis=0, concat_axis=0, tiled=True)

    ratio = jnp.repeat(channel_ratio.reshape(8, 8).T.reshape(64), 2)[None, :]
    filled = lax.dynamic_slice_in_dim(notes[:, 2], me_pf * 16, 16, 1).astype(jnp.int32).reshape(-1)
    patches = make_patches(
        slots, me_pf.reshape(1), filled, recv, notes[:, 0], notes[:, 1], ratio,
        beam_terms.reshape(SG, 2, 8, SUBPIX, SUBPIX), 2 * N_SUB,
    )
    patches = patches.reshape(N_SUB, 256, 256)
    arrived = lax.all_to_all(patches, "sub", split_axis=0, concat_axis=0, tiled=True)
    arrived = arrived.reshape(2 * N_SUB, 128, 256)

    facts = notes[:, 3:7, :SG].astype(jnp.int32)
    at = (2 * me_sub + jnp.arange(2))[None, :, None]
    hit = (facts[:, None, 0] == at).astype(jnp.int32)
    used = jnp.sum(hit, 2).reshape(-1)
    rows = jnp.sum(hit * facts[:, None, 1], 2).reshape(-1)
    cols = jnp.sum(hit * (facts[:, 2] * 128 + facts[:, 3])[:, None], 2).reshape(-1)
    return deposit(used, rows, cols, arrived)


def solution(mesh):
    in_specs = (
        P(None, "pf", "sub"),
        P(None, "sub"),
        P(),
        P("sub", None),
        P("sub"),
        P(("sub", "pf"), None, None, None),
        P(("sub", "pf"), None),
        P(("sub", "pf")),
        P(("sub", "pf")),
    )
    out_specs = P(("sub", "pf"), None, None, None)
    return jax.shard_map(shards, mesh=mesh, in_specs=in_specs, out_specs=out_specs, check_vma=False)
```

```python
import functools

import jax
import jax.numpy as jnp
import numpy as np
from jax import lax
from jax.experimental import pallas as pl
from jax.experimental.pallas import tpu as pltpu
from jax.sharding import PartitionSpec as P

SUBPIX = 64
TILE = 2048
BAND = 96
N_SUB = 32
N_PF = 8
SG = 8
ROWS = 2048
F32 = jnp.float32
BF16 = jnp.bfloat16
MIB = 1 << 20
LIST = 72


def fit_even_odd():
    x = np.cos(np.pi * (np.arange(400) + 0.5) / 400) * 0.125 + 0.125
    r = np.sqrt(x)
    cheb = np.polynomial.chebyshev.Chebyshev
    out = []
    for values, degree in ((np.cos(2 * np.pi * r), 7), (np.sin(2 * np.pi * r) / r, 7)):
        poly = cheb.fit(x, values, degree, domain=[0.0, 0.25]).convert(kind=np.polynomial.Polynomial)
        out.append([float(c) for c in poly.coef])
    return out


COS_COEF, SIN_COEF = fit_even_odd()


def horner(coef, x):
    total = jnp.full_like(x, coef[-1])
    for c in coef[-2::-1]:
        total = total * x + c
    return total


def cos_sin_turns(t):
    r = t - jnp.round(t)
    r2 = r * r
    return horner(COS_COEF, r2), horner(SIN_COEF, r2) * r


def split_hi_lo(x):
    hi = x.astype(BF16)
    return hi, (x - hi.astype(F32)).astype(BF16)


def dft_tables():
    centred = np.arange(SUBPIX) - SUBPIX // 2
    angle = -2.0 * np.pi * ((centred[:, None] * centred[None, :]) % SUBPIX) / SUBPIX
    c, s = np.cos(angle), np.sin(angle)
    right = np.block([[c, s], [-s, c]])
    left = np.block([[c, -s], [s, c]]) / SUBPIX

    def parts(m):
        hi = m.astype(np.float32).astype(BF16)
        lo = (m - hi.astype(np.float64)).astype(np.float32).astype(BF16)
        return hi, lo

    rh, rl = parts(right)
    lh, ll = parts(left)
    ramp = np.cos(2 * np.pi * (np.arange(SUBPIX) + 0.5) / SUBPIX)
    window = 0.55 - 0.45 * ramp
    window = (window[:, None] * window[None, :]).astype(np.float32)
    return np.concatenate([rh, rh], 0), rl, np.concatenate([lh, lh], 1), ll, window


def pick_lanes(source, rows):
    row = lax.broadcasted_iota(jnp.int32, (rows, source.shape[1]), 0)
    return jnp.where(row == source, 1.0, 0.0).astype(BF16)


def dispatch_kernel(
    count_ref, tile_ref, offrow_ref, offcol_ref, vis_ref, place_ref, id_ref, send_ref, slot_scr, placed_scr
):
    count = count_ref[0]
    lane = lax.broadcasted_iota(jnp.int32, (128, 128), 1)
    row_in = lax.broadcasted_iota(jnp.int32, (128, 128), 0)
    lane_f = lane.astype(F32)
    for block in range(ROWS // 128):
        ids = jnp.broadcast_to(id_ref[block : block + 1, :].astype(F32), (128, 128)).T

        def seen(chunk, hits):
            return jnp.where(ids == id_ref[pl.ds(chunk, 1), :].astype(F32), 1.0, hits)

        hits = lax.fori_loop(0, block, seen, jnp.zeros((128, 128), F32))
        here = (ids == id_ref[block : block + 1, :].astype(F32)) & (lane < row_in)
        hits = jnp.where(here, 1.0, hits)
        rank = jnp.max(hits, axis=1, keepdims=True)
        slot = jnp.where(row_in + block * 128 < count, ids * 2.0 + rank, -4096.0)
        slot_scr[block * 128 : (block + 1) * 128, :] = slot - lane_f

    note_row = lax.broadcasted_iota(jnp.int32, (16, 128), 0)
    note_lane = lax.broadcasted_iota(jnp.int32, (16, 128), 1)
    notes = jnp.zeros((16, 128), F32)
    tiles_of = [tile_ref[g, 0] for g in range(SG)]
    for g in range(SG):
        rank = jnp.int32(0)
        for h in range(g):
            rank = rank + (tiles_of[h] == tiles_of[g]).astype(jnp.int32)
        col = offcol_ref[g]
        for at, value in enumerate((tiles_of[g] * 2 + rank, offrow_ref[g], col >> 7, col & 127)):
            notes = jnp.where((note_row == 3 + at) & (note_lane == g), value.astype(F32), notes)

    order = lax.broadcasted_iota(jnp.int32, (64, 64), 0)
    order = (order & 7) * 8 + (order >> 3)
    order = jnp.where(lax.broadcasted_iota(jnp.int32, (64, 64), 1) == order, 1.0, 0.0).astype(BF16)
    vis = vis_ref[...].astype(F32).reshape(64, ROWS).astype(BF16)
    vis = jnp.dot(order, vis, preferred_element_type=F32)
    place = place_ref[...].astype(F32)
    extra_row = lax.broadcasted_iota(jnp.int32, (16, ROWS), 0)
    extra = jnp.where(extra_row == 2, 1.0, 0.0)
    extra = jnp.where(extra_row == 0, place[0:1], jnp.where(extra_row == 1, place[1:2], extra))
    data = jnp.concatenate([vis, extra], 0).astype(BF16)

    def one_owner(owner, carry):
        rel = slot_scr[...]
        first = (owner * 256).astype(F32)
        picks = jnp.concatenate(
            [
                jnp.where(rel == first, 1.0, 0.0).astype(BF16),
                jnp.where(rel == first + 128.0, 1.0, 0.0).astype(BF16),
            ],
            1,
        )
        placed = jnp.dot(data, picks, preferred_element_type=F32)
        halves = (placed[:, :128], placed[:, 128:])
        for c in range(8):
            both = jnp.concatenate([part[c * 8 : (c + 1) * 8] for part in halves], 0)
            placed_scr[c, pl.ds(pl.multiple_of(owner * 16, 16), 16), :] = both.astype(BF16)
        for k, part in enumerate(halves):
            send_ref[owner * 2 + k, 64:80] = (part[64:80] + notes).astype(BF16)
        return carry

    lax.fori_loop(0, N_SUB // 2, one_owner, 0)

    by_channel = jnp.concatenate([placed_scr[c] for c in range(8)], 1)
    out_lane = lax.broadcasted_iota(jnp.int32, (1, 256), 1)
    for pair in range(N_PF // 2):
        channel, slot = (out_lane >> 4) & 7, out_lane & 15
        source = channel * 128 + (pair * 2 + (out_lane >> 7)) * 16 + slot
        moved = jnp.dot(by_channel, pick_lanes(source, 1024), preferred_element_type=F32)
        for d in range(N_SUB):
            rows = moved[d * 8 : (d + 1) * 8]
            both = jnp.concatenate([rows[:, :128], rows[:, 128:]], 0)
            send_ref[d, pair * 16 : pair * 16 + 16] = both.astype(BF16)


def dispatch(count, tile, offset_rows, offset_cols, vis, place, ids):
    vmem = pl.BlockSpec(memory_space=pltpu.VMEM)
    smem = pl.BlockSpec(memory_space=pltpu.SMEM)
    return pl.pallas_call(
        dispatch_kernel,
        out_shape=jax.ShapeDtypeStruct((N_SUB, 80, 128), BF16),
        in_specs=[smem] * 4 + [vmem] * 3,
        out_specs=vmem,
        scratch_shapes=[pltpu.VMEM((ROWS, 128), F32), pltpu.VMEM((8, 256, 128), BF16)],
        compiler_params=pltpu.CompilerParams(vmem_limit_bytes=48 * MIB),
        name="dispatch",
    )(count, tile, offset_rows, offset_cols, vis, place, ids)


def cmul(a, b):
    return a[0] * b[0] - a[1] * b[1], a[0] * b[1] + a[1] * b[0]


def conj_mul(a, b):
    return a[0] * b[0] + a[1] * b[1], a[0] * b[1] - a[1] * b[0]


def cadd(a, b):
    return a[0] + b[0], a[1] + b[1]


def corrected_image(image, left, right, window):
    middle = {}
    for i in range(2):
        for j in range(2):
            middle[i, j] = cadd(conj_mul(left[i], image[j]), conj_mul(left[2 + i], image[2 + j]))
    out = []
    for i in range(2):
        for j in range(2):
            re, im = cadd(cmul(middle[i, 0], right[j]), cmul(middle[i, 1], right[2 + j]))
            out.append((re * window, im * window))
    return out


def phases(base_turns, tile_turns):
    cb, sb = cos_sin_turns(base_turns)
    ca, sa = cos_sin_turns(tile_turns)
    cos_out, sin_out = [], []
    for a in range(8):
        c, s = ca[a : a + 1], sa[a : a + 1]
        cos_out.append(cb * c - sb * s)
        sin_out.append(cb * s + sb * c)
    return jnp.concatenate(cos_out, 0), jnp.concatenate(sin_out, 0)


def subgrid_kernel(
    plan_ref, pf_ref, note_ref, recv_ref, notes_ref, ratio_ref, beam_ref, rt2_ref, rtl_ref, lt2_ref, ltl_ref,
    window_ref, send_ref, send2_ref, vis_scr, u_scr, v_scr, place_scr, list_scr, total_scr, patch_scr, sems,
):
    tile_lane = lax.broadcasted_iota(jnp.int32, (8, 128), 1)
    odd = (tile_lane & 1) == 1
    base = pf_ref[0] * 16

    def read_place(source, carry):
        place = notes_ref[source].astype(F32)
        place_scr[0, pl.ds(source, 1)] = place[0:1]
        place_scr[1, pl.ds(source, 1)] = place[1:2]
        return carry

    lax.fori_loop(0, N_SUB, read_place, 0)

    by_sender = jnp.concatenate([recv_ref[p] for p in range(N_PF)], 1)
    out_lane = lax.broadcasted_iota(jnp.int32, (1, 256), 1)
    from_lane = ((out_lane >> 1) & 7) * 128 + ((out_lane >> 4) & 7) * 16 + (out_lane >> 7)

    def regroup(g, carry):
        picks = pick_lanes(from_lane + g * 2, 1024)
        moved = jnp.dot(by_sender, picks, preferred_element_type=F32)
        for j in range(2):
            block = moved[:, j * 128 : (j + 1) * 128].reshape(N_SUB, 8, 128)
            vis_scr[pl.ds(g * 64 + j * 32, N_SUB)] = block
        count = jnp.int32(0)
        for j in range(2):
            for source in range(N_SUB):
                list_scr[g * LIST + count] = g * 64 + (j * 32 + source)
                count = count + note_ref[source * 5, base + g * 2 + j]
        for k in range(8):
            list_scr[g * LIST + count + k] = 512
        list_scr[SG * LIST + g] = count
        return carry

    lax.fori_loop(0, SG, regroup, 0)
    vis_scr[512] = jnp.zeros((8, 128), F32)

    ratio = ratio_ref[...]
    for part, scr in ((0, u_scr), (1, v_scr)):
        mine = pltpu.roll(place_scr[part], lax.rem(128 - base, 128), 1)
        for g in range(SG):
            for j in range(2):
                k = g * 2 + j
                scr[g * 64 + j * 32 : g * 64 + j * 32 + 32, :] = mine[:, k : k + 1] * ratio
        scr[512:520, :] = jnp.zeros((8, 128), F32)

    units = 4
    eight = lax.broadcasted_iota(jnp.int32, (8, 128 * units), 0).astype(F32)
    base_x = eight * (1.0 / 64.0)
    tile_x = (eight - 4.0) * (1.0 / 8.0)
    half_lane = lax.broadcasted_iota(jnp.int32, (SUBPIX, 128), 1) < SUBPIX
    window = window_ref[...]

    def post(g, act):
        slot = plan_ref[g]

        @pl.when(slot < N_SUB)
        def _():
            act(pltpu.make_async_copy(patch_scr.at[g], send_ref.at[slot], sems.at[g]))

        @pl.when(slot >= N_SUB)
        def _():
            act(pltpu.make_async_copy(patch_scr.at[g], send2_ref.at[slot - N_SUB], sems.at[g]))

    def one_subgrid(g, carry):
        def accumulate(step, inner):
            first = g * LIST + step * (2 * units)
            picked = [list_scr[first + k] for k in range(2 * units)]

            def lanes(load, mask):
                return jnp.concatenate(
                    [
                        jnp.where(mask, load(picked[2 * k + 1]), load(picked[2 * k]))
                        for k in range(units)
                    ],
                    1,
                )

            u = lanes(lambda i: u_scr[pl.ds(i, 1), :], odd[0:1])
            v = lanes(lambda i: v_scr[pl.ds(i, 1), :], odd[0:1])
            vis = lanes(lambda i: vis_scr[i], odd)
            cos_u, sin_u = phases(u * base_x, u * tile_x)
            cos_v, sin_v = phases(v * base_x, v * tile_x)
            rows = []
            for q in range(4):
                re, im = vis[2 * q : 2 * q + 1], vis[2 * q + 1 : 2 * q + 2]
                rows.append((re * cos_u - im * sin_u).astype(BF16))
                rows.append((re * sin_u + im * cos_u).astype(BF16))
            left = jnp.concatenate(rows, 0)
            right = jnp.concatenate([cos_v.astype(BF16), sin_v.astype(BF16)], 0)
            total_scr[g] += lax.dot_general(
                left, right, (((1,), (1,)), ((), ())), preferred_element_type=F32
            )
            return inner

        steps = (list_scr[SG * LIST + g] + (2 * units - 1)) // (2 * units)
        total_scr[g] = jnp.zeros((512, 128), F32)
        lax.fori_loop(0, steps, accumulate, 0)
        return carry

    lax.fori_loop(0, SG, one_subgrid, 0)

    def one_patch(g):
        total = total_scr[g]
        image = []
        for q in range(4):
            re = total[q * 128 : q * 128 + 64]
            im = total[q * 128 + 64 : q * 128 + 128]
            image.append((re[:, :64] - im[:, 64:], re[:, 64:] + im[:, :64]))
        beams = [
            [
                (beam_ref[g, side, 2 * e].astype(F32), beam_ref[g, side, 2 * e + 1].astype(F32))
                for e in range(4)
            ]
            for side in range(2)
        ]
        pieces = corrected_image(image, beams[0], beams[1], window)
        stacked = jnp.concatenate([jnp.concatenate([re, im], 1) for re, im in pieces], 0)
        hi, lo = split_hi_lo(stacked)
        mid = jnp.dot(jnp.concatenate([hi, lo], 1), rt2_ref[...], preferred_element_type=F32)
        mid = mid + jnp.dot(hi, rtl_ref[...], preferred_element_type=F32)
        mids = [mid[q * 64 : (q + 1) * 64] for q in range(4)]
        upper, lower = [], []
        for q in (0, 2):
            upper.append(jnp.where(half_lane, mids[q], pltpu.roll(mids[q + 1], 64, 1)))
            lower.append(jnp.where(half_lane, pltpu.roll(mids[q], 64, 1), mids[q + 1]))
        both = jnp.concatenate([jnp.concatenate(upper, 1), jnp.concatenate(lower, 1)], 0)
        hi, lo = split_hi_lo(both)
        out = jnp.dot(lt2_ref[...], jnp.concatenate([hi, lo], 0), preferred_element_type=F32)
        out = out + jnp.dot(ltl_ref[...], hi, preferred_element_type=F32)
        patch_scr[g] = out.astype(BF16)
        post(g, lambda copy: copy.start())

    def two_patches(pair, carry):
        one_patch(pair * 2)
        one_patch(pair * 2 + 1)
        return carry

    lax.fori_loop(0, SG // 2, two_patches, 0)

    def finish(g, carry):
        post(g, lambda copy: copy.wait())
        return carry

    lax.fori_loop(0, SG, finish, 0)


def make_patches(plan, pf_index, ints, recv, notes, ratio, beams):
    vmem = pl.BlockSpec(memory_space=pltpu.VMEM)
    smem = pl.BlockSpec(memory_space=pltpu.SMEM)
    return pl.pallas_call(
        subgrid_kernel,
        out_shape=(jax.ShapeDtypeStruct((N_SUB, 128, 256), BF16),) * 2,
        in_specs=[smem] * 3 + [vmem] * 9,
        out_specs=(pl.BlockSpec(memory_space=pl.ANY),) * 2,
        scratch_shapes=[
            pltpu.VMEM((SG * 64 + 1, 8, 128), F32),
            pltpu.VMEM((SG * 64 + 8, 128), F32),
            pltpu.VMEM((SG * 64 + 8, 128), F32),
            pltpu.VMEM((2, N_SUB, 128), F32),
            pltpu.SMEM((SG * LIST + SG,), jnp.int32),
            pltpu.VMEM((SG, 512, 128), F32),
            pltpu.VMEM((SG, 128, 256), BF16),
            pltpu.SemaphoreType.DMA((SG,)),
        ],
        compiler_params=pltpu.CompilerParams(vmem_limit_bytes=48 * MIB),
        name="subgrids",
    )(plan, pf_index, ints, recv, notes, ratio, beams, *dft_tables())


HELPERS = 4
RELAYED = 4
AT_BAD = 8
AT_RELAY = 16
AT_USED = 32
DUMP = 80
AT_ROW = AT_USED + DUMP + 8
AT_COL = AT_ROW + DUMP + 8
PLAN = AT_COL + DUMP + 8
AT_SECOND = N_SUB + HELPERS * RELAYED


def neighbour(tile, k):
    if k < 2:
        return (tile & 28) | ((tile + (1, 3)[k]) & 3)
    return (tile + (4, 28)[k - 2]) & 31


def plan_kernel(me_ref, note_ref, plan_ref, load_scr, mask_scr):
    me = me_ref[0]

    def clear(i, carry):
        for k in range(8):
            plan_ref[i * 8 + k] = 0
        return carry

    def clear_load(i, carry):
        for k in range(8):
            load_scr[i * 8 + k] = 0
        return carry

    lax.fori_loop(0, PLAN // 8, clear, 0)
    lax.fori_loop(0, HELPERS * N_SUB // 8, clear_load, 0)
    for i in range(HELPERS * RELAYED):
        plan_ref[AT_RELAY + i] = -1
    for g in range(SG):
        plan_ref[g] = note_ref[me * 5 + 1, g] >> 1

    def note(entry, used, source, g):
        plan_ref[AT_USED + entry] = used
        plan_ref[AT_ROW + entry] = note_ref[source * 5 + 2, g]
        plan_ref[AT_COL + entry] = note_ref[source * 5 + 3, g] * 128 + note_ref[source * 5 + 4, g]

    def seconds(source):
        mask = jnp.int32(0)
        for g in range(SG):
            mask = mask | (jnp.int32(1) << (note_ref[source * 5 + 1, g] >> 1))
        mask_scr[0] = mask

        def one(g, carry):
            slot = note_ref[source * 5 + 1, g]

            @pl.when((slot & 1) == 1)
            def _():
                tile = slot >> 1
                busy = mask_scr[0]
                best, helper, load = jnp.int32(-1), jnp.int32(0), jnp.int32(RELAYED)
                for k in range(HELPERS):
                    via = neighbour(tile, k)
                    held = load_scr[k * N_SUB + tile]
                    better = (((busy >> via) & 1) == 0) & (held < load)
                    best = jnp.where(better, k, best)
                    helper = jnp.where(better, via, helper)
                    load = jnp.where(better, held, load)

                @pl.when(best >= 0)
                def _():
                    mask_scr[0] = busy | (jnp.int32(1) << helper)
                    load_scr[best * N_SUB + tile] = load + 1
                    place = best * RELAYED + load

                    @pl.when(source == me)
                    def _():
                        plan_ref[g] = helper

                    @pl.when(helper == me)
                    def _():
                        plan_ref[AT_RELAY + place] = source

                    @pl.when(tile == me)
                    def _():
                        note(N_SUB + place, 1, source, g)

                @pl.when(best < 0)
                def _():
                    plan_ref[AT_BAD] = 1

                    @pl.when(source == me)
                    def _():
                        plan_ref[g] = N_SUB + tile

                    @pl.when(tile == me)
                    def _():
                        note(AT_SECOND + source, 1, source, g)

            return carry

        lax.fori_loop(0, SG, one, 0)

    def one_source(source, carry):
        which, any_second = jnp.int32(0), jnp.int32(0)
        for g in range(SG):
            slot = note_ref[source * 5 + 1, g]
            which = jnp.where(slot == 2 * me, g + 1, which)
            any_second = any_second | (slot & 1)
        note(source, jnp.minimum(which, 1), source, jnp.maximum(which - 1, 0))

        @pl.when(any_second > 0)
        def _():
            seconds(source)

        return carry

    lax.fori_loop(0, N_SUB, one_source, 0)


def make_plan(me, ints):
    smem = pl.BlockSpec(memory_space=pltpu.SMEM)
    return pl.pallas_call(
        plan_kernel,
        out_shape=jax.ShapeDtypeStruct((PLAN,), jnp.int32),
        in_specs=[smem] * 2,
        out_specs=smem,
        scratch_shapes=[
            pltpu.SMEM((HELPERS * N_SUB,), jnp.int32),
            pltpu.SMEM((1,), jnp.int32),
        ],
        name="plan",
    )(me, ints)


def relay_kernel(plan_ref, arrived_ref, *outs):
    out_refs, sems = outs[:HELPERS], outs[HELPERS]

    def each(act):
        for k in range(HELPERS):
            for c in range(RELAYED):
                source = plan_ref[AT_RELAY + k * RELAYED + c]

                @pl.when(source >= 0)
                def _(k=k, c=c, source=source):
                    act(
                        pltpu.make_async_copy(
                            arrived_ref.at[source], out_refs[k].at[c], sems.at[k * RELAYED + c]
                        )
                    )

    each(lambda copy: copy.start())
    each(lambda copy: copy.wait())


def relay(plan, arrived):
    hbm = pl.BlockSpec(memory_space=pl.ANY)
    return pl.pallas_call(
        relay_kernel,
        out_shape=(jax.ShapeDtypeStruct((RELAYED, 128, 256), BF16),) * HELPERS,
        in_specs=[pl.BlockSpec(memory_space=pltpu.SMEM), hbm],
        out_specs=(hbm,) * HELPERS,
        scratch_shapes=[pltpu.SemaphoreType.DMA((HELPERS * RELAYED,))],
        name="relay",
    )(plan, arrived)


def deposit_kernel(firsts, plan_ref, *refs):
    recv_refs, out_ref = refs[:-1], refs[-1]
    out_ref[...] = jnp.zeros_like(out_ref)
    tall = SUBPIX + 8
    lane = lax.broadcasted_iota(jnp.int32, (2 * tall, 256), 1)
    blank = jnp.zeros((8, 256), F32)

    for first, recv_ref in zip(firsts, recv_refs):

        def one_slot(slot, carry, first=first, recv_ref=recv_ref):
            @pl.when(plan_ref[AT_USED + first + slot] > 0)
            def _():
                row = plan_ref[AT_ROW + first + slot]
                col = plan_ref[AT_COL + first + slot]
                top = pl.multiple_of(jnp.minimum((row // 8) * 8, BAND - tall), 8)
                start = pl.multiple_of(jnp.minimum((col // 128) * 128, TILE - 256), 128)
                shift = col - start
                patch = recv_ref[slot].astype(F32)
                patch = jnp.concatenate([patch[:SUBPIX], blank, patch[SUBPIX:], blank], 0)
                patch = pltpu.roll(patch, row - top, 0)
                inside = (lane >= shift) & (lane < shift + SUBPIX)
                for q in range(4):
                    moved = pltpu.roll(patch, lax.rem(shift + 256 - q * 64, 256), 1)
                    moved = jnp.where(inside, moved, 0.0)
                    for s in range(2):
                        spot = (0, 2 * q + s, pl.ds(top, tall), pl.ds(start, 256))
                        out_ref[spot] += moved[s * tall : (s + 1) * tall]

            return carry

        lax.fori_loop(0, recv_ref.shape[0], one_slot, 0)


def deposit(plan, firsts, patches):
    vmem = pl.BlockSpec(memory_space=pltpu.VMEM)
    smem = pl.BlockSpec(memory_space=pltpu.SMEM)
    return pl.pallas_call(
        functools.partial(deposit_kernel, firsts),
        out_shape=jax.ShapeDtypeStruct((1, 8, BAND, TILE), F32),
        in_specs=[smem] + [vmem] * len(patches),
        out_specs=vmem,
        compiler_params=pltpu.CompilerParams(vmem_limit_bytes=48 * MIB),
        name="deposit",
    )(plan, *patches)


def shards(
    visibilities,
    row_positions,
    channel_ratio,
    row_subgrid,
    row_count,
    beam_terms,
    subgrid_tile,
    offset_rows,
    offset_cols,
):
    me_sub = lax.axis_index("sub")
    me_pf = lax.axis_index("pf")
    send = dispatch(
        row_count, subgrid_tile, offset_rows, offset_cols, visibilities, row_positions,
        row_subgrid.reshape(ROWS // 128, 128),
    )
    recv = lax.all_to_all(send, "sub", split_axis=0, concat_axis=0, tiled=True)
    notes = recv[:, 64:80]
    recv = jnp.transpose(recv[:, :64].reshape(N_SUB, N_PF, 8, 128), (1, 0, 2, 3))
    recv = recv.reshape(N_PF, N_SUB * 8, 128)
    recv = lax.all_to_all(recv, "pf", split_axis=0, concat_axis=0, tiled=True)

    ratio = jnp.repeat(channel_ratio.reshape(8, 8).T.reshape(64), 2)[None, :]
    ints = notes[:, 2:7].astype(jnp.int32).reshape(N_SUB * 5, 128)
    plan = make_plan(me_sub.reshape(1), ints)
    bad = jnp.full((N_PF, 8, 128), plan[AT_BAD].astype(F32))
    bad = lax.all_to_all(bad, "pf", split_axis=0, concat_axis=0, tiled=True)
    bad = jnp.max(bad[:, 0, 0]) > 0
    patches, second = make_patches(
        plan, me_pf.reshape(1), ints, recv, notes, ratio,
        beam_terms.reshape(SG, 2, 8, SUBPIX, SUBPIX),
    )
    arrived = lax.all_to_all(patches, "sub", split_axis=0, concat_axis=0, tiled=True)
    relayed = [
        lax.ppermute(block, "sub", [(neighbour(t, k), t) for t in range(N_SUB)])
        for k, block in enumerate(relay(plan, arrived))
    ]
    firsts = (0,) + tuple(N_SUB + k * RELAYED for k in range(HELPERS))

    def with_second(plan, second, *blocks):
        late = lax.all_to_all(second, "sub", split_axis=0, concat_axis=0, tiled=True)
        return deposit(plan, firsts + (AT_SECOND,), blocks + (late,))

    def without(plan, second, *blocks):
        return deposit(plan, firsts, blocks)

    return lax.cond(bad, with_second, without, plan, second, arrived, *relayed)


def solution(mesh):
    in_specs = (
        P(None, "pf", "sub"),
        P(None, "sub"),
        P(),
        P("sub", None),
        P("sub"),
        P(("sub", "pf"), None, None, None),
        P(("sub", "pf"), None),
        P(("sub", "pf")),
        P(("sub", "pf")),
    )
    out_specs = P(("sub", "pf"), None, None, None)
    return jax.shard_map(shards, mesh=mesh, in_specs=in_specs, out_specs=out_specs, check_vma=False)
```

```python
import functools

import jax
import jax.numpy as jnp
import numpy as np
from jax import lax
from jax.experimental import pallas as pl
from jax.experimental.pallas import tpu as pltpu
from jax.sharding import PartitionSpec as P

SUBPIX = 64
TILE = 2048
BAND = 96
N_SUB = 32
N_PF = 8
SG = 8
ROWS = 2048
F32 = jnp.float32
BF16 = jnp.bfloat16
MIB = 1 << 20
LIST = 80


def fit_even_odd():
    x = np.cos(np.pi * (np.arange(400) + 0.5) / 400) * 0.125 + 0.125
    r = np.sqrt(x)
    cheb = np.polynomial.chebyshev.Chebyshev
    out = []
    for values, degree in ((np.cos(2 * np.pi * r), 7), (np.sin(2 * np.pi * r) / r, 7)):
        poly = cheb.fit(x, values, degree, domain=[0.0, 0.25]).convert(kind=np.polynomial.Polynomial)
        out.append([float(c) for c in poly.coef])
    return out


COS_COEF, SIN_COEF = fit_even_odd()


def horner(coef, x):
    total = jnp.full_like(x, coef[-1])
    for c in coef[-2::-1]:
        total = total * x + c
    return total


def cos_sin_turns(t):
    r = t - jnp.round(t)
    r2 = r * r
    return horner(COS_COEF, r2), horner(SIN_COEF, r2) * r


def split_hi_lo(x):
    hi = x.astype(BF16)
    return hi, (x - hi.astype(F32)).astype(BF16)


def dft_tables():
    centred = np.arange(SUBPIX) - SUBPIX // 2
    angle = -2.0 * np.pi * ((centred[:, None] * centred[None, :]) % SUBPIX) / SUBPIX
    c, s = np.cos(angle), np.sin(angle)
    right = np.block([[c, s], [-s, c]])
    left = np.block([[c, -s], [s, c]]) / SUBPIX

    def parts(m):
        hi = m.astype(np.float32).astype(BF16)
        lo = (m - hi.astype(np.float64)).astype(np.float32).astype(BF16)
        return hi, lo

    rh, rl = parts(right)
    lh, ll = parts(left)
    ramp = np.cos(2 * np.pi * (np.arange(SUBPIX) + 0.5) / SUBPIX)
    window = 0.55 - 0.45 * ramp
    window = (window[:, None] * window[None, :]).astype(np.float32)
    return np.concatenate([rh, rh], 0), rl, np.concatenate([lh, lh], 1), ll, window


def pick_lanes(source, rows):
    row = lax.broadcasted_iota(jnp.int32, (rows, source.shape[1]), 0)
    return jnp.where(row == source, 1.0, 0.0).astype(BF16)


def dispatch_kernel(
    scalar_ref, vis_ref, place_ref, id_ref, send_ref, slot_scr, placed_scr
):
    count = scalar_ref[3 * SG]
    lane = lax.broadcasted_iota(jnp.int32, (128, 128), 1)
    row_in = lax.broadcasted_iota(jnp.int32, (128, 128), 0)
    lane_f = lane.astype(F32)
    for block in range(ROWS // 128):
        ids = jnp.broadcast_to(id_ref[block : block + 1, :].astype(F32), (128, 128)).T

        def seen(chunk, hits):
            return jnp.where(ids == id_ref[pl.ds(chunk, 1), :].astype(F32), 1.0, hits)

        hits = lax.fori_loop(0, block, seen, jnp.zeros((128, 128), F32))
        here = (ids == id_ref[block : block + 1, :].astype(F32)) & (lane < row_in)
        hits = jnp.where(here, 1.0, hits)
        rank = jnp.max(hits, axis=1, keepdims=True)
        slot = jnp.where(row_in + block * 128 < count, ids * 2.0 + rank, -4096.0)
        slot_scr[block * 128 : (block + 1) * 128, :] = slot - lane_f

    note_row = lax.broadcasted_iota(jnp.int32, (16, 128), 0)
    note_lane = lax.broadcasted_iota(jnp.int32, (16, 128), 1)
    notes = jnp.zeros((16, 128), F32)
    tiles_of = [scalar_ref[g] for g in range(SG)]
    for g in range(SG):
        rank = jnp.int32(0)
        for h in range(g):
            rank = rank + (tiles_of[h] == tiles_of[g]).astype(jnp.int32)
        row, col = scalar_ref[SG + g], scalar_ref[2 * SG + g]
        for at, value in enumerate((tiles_of[g] * 2 + rank, row, col >> 7, col & 127)):
            notes = jnp.where((note_row == 3 + at) & (note_lane == g), value.astype(F32), notes)

    order = lax.broadcasted_iota(jnp.int32, (64, 64), 0)
    order = (order & 7) * 8 + (order >> 3)
    order = jnp.where(lax.broadcasted_iota(jnp.int32, (64, 64), 1) == order, 1.0, 0.0).astype(BF16)
    vis = vis_ref[...].astype(F32).reshape(64, ROWS).astype(BF16)
    vis = jnp.dot(order, vis, preferred_element_type=F32)
    place = place_ref[...].astype(F32)
    extra_row = lax.broadcasted_iota(jnp.int32, (16, ROWS), 0)
    extra = jnp.where(extra_row == 2, 1.0, 0.0)
    extra = jnp.where(extra_row == 0, place[0:1], jnp.where(extra_row == 1, place[1:2], extra))
    data = jnp.concatenate([vis, extra], 0).astype(BF16)

    def one_owner(owner, carry):
        rel = slot_scr[...]
        first = (owner * 256).astype(F32)
        picks = jnp.concatenate(
            [
                jnp.where(rel == first, 1.0, 0.0).astype(BF16),
                jnp.where(rel == first + 128.0, 1.0, 0.0).astype(BF16),
            ],
            1,
        )
        placed = jnp.dot(data, picks, preferred_element_type=F32)
        halves = (placed[:, :128], placed[:, 128:])
        for c in range(8):
            both = jnp.concatenate([part[c * 8 : (c + 1) * 8] for part in halves], 0)
            placed_scr[c, pl.ds(pl.multiple_of(owner * 16, 16), 16), :] = both.astype(BF16)
        for k, part in enumerate(halves):
            send_ref[owner * 2 + k, 64:80] = (part[64:80] + notes).astype(BF16)
        return carry

    lax.fori_loop(0, N_SUB // 2, one_owner, 0)

    by_channel = jnp.concatenate([placed_scr[c] for c in range(8)], 1)
    out_lane = lax.broadcasted_iota(jnp.int32, (1, 256), 1)
    for pair in range(N_PF // 2):
        channel, slot = (out_lane >> 4) & 7, out_lane & 15
        source = channel * 128 + (pair * 2 + (out_lane >> 7)) * 16 + slot
        moved = jnp.dot(by_channel, pick_lanes(source, 1024), preferred_element_type=F32)
        for d in range(N_SUB):
            rows = moved[d * 8 : (d + 1) * 8]
            both = jnp.concatenate([rows[:, :128], rows[:, 128:]], 0)
            send_ref[d, pair * 16 : pair * 16 + 16] = both.astype(BF16)


def dispatch(scalars, vis, place, ids):
    vmem = pl.BlockSpec(memory_space=pltpu.VMEM)
    smem = pl.BlockSpec(memory_space=pltpu.SMEM)
    return pl.pallas_call(
        dispatch_kernel,
        out_shape=jax.ShapeDtypeStruct((N_SUB, 80, 128), BF16),
        in_specs=[smem] + [vmem] * 3,
        out_specs=vmem,
        scratch_shapes=[pltpu.VMEM((ROWS, 128), F32), pltpu.VMEM((8, 256, 128), BF16)],
        compiler_params=pltpu.CompilerParams(vmem_limit_bytes=48 * MIB),
        name="dispatch",
    )(scalars, vis, place, ids)


def cmul(a, b):
    return a[0] * b[0] - a[1] * b[1], a[0] * b[1] + a[1] * b[0]


def conj_mul(a, b):
    return a[0] * b[0] + a[1] * b[1], a[0] * b[1] - a[1] * b[0]


def cadd(a, b):
    return a[0] + b[0], a[1] + b[1]


def corrected_image(image, left, right, window):
    middle = {}
    for i in range(2):
        for j in range(2):
            middle[i, j] = cadd(conj_mul(left[i], image[j]), conj_mul(left[2 + i], image[2 + j]))
    out = []
    for i in range(2):
        for j in range(2):
            re, im = cadd(cmul(middle[i, 0], right[j]), cmul(middle[i, 1], right[2 + j]))
            out.append((re * window, im * window))
    return out


def phases(base_turns, tile_turns):
    cb, sb = cos_sin_turns(base_turns)
    ca, sa = cos_sin_turns(tile_turns)
    cos_out, sin_out = [], []
    for a in range(8):
        c, s = ca[a : a + 1], sa[a : a + 1]
        cos_out.append(cb * c - sb * s)
        sin_out.append(cb * s + sb * c)
    return jnp.concatenate(cos_out, 0), jnp.concatenate(sin_out, 0)


def subgrid_kernel(
    plan_ref, pf_ref, note_ref, recv_ref, notes_ref, ratio_ref, beam_ref, rt2_ref, rtl_ref, lt2_ref, ltl_ref,
    window_ref, send_ref, send2_ref, vis_scr, u_scr, v_scr, place_scr, list_scr, total_scr, patch_scr, sems,
):
    tile_lane = lax.broadcasted_iota(jnp.int32, (8, 128), 1)
    odd = (tile_lane & 1) == 1
    base = pf_ref[0] * 16

    def read_place(source, carry):
        place = notes_ref[source, 64:80].astype(F32)
        place_scr[0, pl.ds(source, 1)] = place[0:1]
        place_scr[1, pl.ds(source, 1)] = place[1:2]
        return carry

    lax.fori_loop(0, N_SUB, read_place, 0)

    by_sender = jnp.concatenate([recv_ref[p] for p in range(N_PF)], 1)
    out_lane = lax.broadcasted_iota(jnp.int32, (1, 256), 1)
    from_lane = ((out_lane >> 1) & 7) * 128 + ((out_lane >> 4) & 7) * 16 + (out_lane >> 7)

    def regroup(g, carry):
        picks = pick_lanes(from_lane + g * 2, 1024)
        moved = jnp.dot(by_sender, picks, preferred_element_type=F32)
        for j in range(2):
            block = moved[:, j * 128 : (j + 1) * 128].reshape(N_SUB, 8, 128)
            vis_scr[pl.ds(g * 64 + j * 32, N_SUB)] = block
        count = jnp.int32(0)
        for j in range(2):
            for source in range(N_SUB):
                list_scr[g * LIST + count] = g * 64 + (j * 32 + source)
                count = count + note_ref[source * 5, base + g * 2 + j]
        for k in range(16):
            list_scr[g * LIST + count + k] = 512
        list_scr[SG * LIST + g] = count
        return carry

    lax.fori_loop(0, SG, regroup, 0)
    vis_scr[512] = jnp.zeros((8, 128), F32)

    ratio = ratio_ref[...]
    for part, scr in ((0, u_scr), (1, v_scr)):
        mine = pltpu.roll(place_scr[part], lax.rem(128 - base, 128), 1)
        for g in range(SG):
            for j in range(2):
                k = g * 2 + j
                scr[g * 64 + j * 32 : g * 64 + j * 32 + 32, :] = mine[:, k : k + 1] * ratio
        scr[512:520, :] = jnp.zeros((8, 128), F32)

    units = 8
    eight = lax.broadcasted_iota(jnp.int32, (8, 128 * units), 0).astype(F32)
    base_x = eight * (1.0 / 64.0)
    tile_x = (eight - 4.0) * (1.0 / 8.0)
    half_lane = lax.broadcasted_iota(jnp.int32, (SUBPIX, 128), 1) < SUBPIX
    window = window_ref[...]

    def post(g, act):
        slot = plan_ref[g]

        @pl.when(slot < N_SUB)
        def _():
            act(pltpu.make_async_copy(patch_scr.at[g], send_ref.at[slot], sems.at[g]))

        @pl.when(slot >= N_SUB)
        def _():
            act(pltpu.make_async_copy(patch_scr.at[g], send2_ref.at[slot - N_SUB], sems.at[g]))

    def one_subgrid(g, carry):
        def accumulate(step, inner):
            first = g * LIST + step * (2 * units)
            picked = [list_scr[first + k] for k in range(2 * units)]

            def lanes(load, mask):
                return jnp.concatenate(
                    [
                        jnp.where(mask, load(picked[2 * k + 1]), load(picked[2 * k]))
                        for k in range(units)
                    ],
                    1,
                )

            u = lanes(lambda i: u_scr[pl.ds(i, 1), :], odd[0:1])
            v = lanes(lambda i: v_scr[pl.ds(i, 1), :], odd[0:1])
            vis = lanes(lambda i: vis_scr[i], odd)
            cos_u, sin_u = phases(u * base_x, u * tile_x)
            cos_v, sin_v = phases(v * base_x, v * tile_x)
            rows = []
            for q in range(4):
                re, im = vis[2 * q : 2 * q + 1], vis[2 * q + 1 : 2 * q + 2]
                rows.append((re * cos_u - im * sin_u).astype(BF16))
                rows.append((re * sin_u + im * cos_u).astype(BF16))
            left = jnp.concatenate(rows, 0)
            right = jnp.concatenate([cos_v.astype(BF16), sin_v.astype(BF16)], 0)
            total_scr[g] += lax.dot_general(
                left, right, (((1,), (1,)), ((), ())), preferred_element_type=F32
            )
            return inner

        steps = (list_scr[SG * LIST + g] + (2 * units - 1)) // (2 * units)
        total_scr[g] = jnp.zeros((512, 128), F32)
        lax.fori_loop(0, steps, accumulate, 0)
        return carry

    lax.fori_loop(0, SG, one_subgrid, 0)

    def one_patch(g):
        total = total_scr[g]
        image = []
        for q in range(4):
            re = total[q * 128 : q * 128 + 64]
            im = total[q * 128 + 64 : q * 128 + 128]
            image.append((re[:, :64] - im[:, 64:], re[:, 64:] + im[:, :64]))
        beams = [
            [
                (beam_ref[g, side, 2 * e].astype(F32), beam_ref[g, side, 2 * e + 1].astype(F32))
                for e in range(4)
            ]
            for side in range(2)
        ]
        pieces = corrected_image(image, beams[0], beams[1], window)
        stacked = jnp.concatenate([jnp.concatenate([re, im], 1) for re, im in pieces], 0)
        hi, lo = split_hi_lo(stacked)
        mid = jnp.dot(jnp.concatenate([hi, lo], 1), rt2_ref[...], preferred_element_type=F32)
        mid = mid + jnp.dot(hi, rtl_ref[...], preferred_element_type=F32)
        mids = [mid[q * 64 : (q + 1) * 64] for q in range(4)]
        upper, lower = [], []
        for q in (0, 2):
            upper.append(jnp.where(half_lane, mids[q], pltpu.roll(mids[q + 1], 64, 1)))
            lower.append(jnp.where(half_lane, pltpu.roll(mids[q], 64, 1), mids[q + 1]))
        both = jnp.concatenate([jnp.concatenate(upper, 1), jnp.concatenate(lower, 1)], 0)
        hi, lo = split_hi_lo(both)
        out = jnp.dot(lt2_ref[...], jnp.concatenate([hi, lo], 0), preferred_element_type=F32)
        out = out + jnp.dot(ltl_ref[...], hi, preferred_element_type=F32)
        patch_scr[g] = out.astype(BF16)
        post(g, lambda copy: copy.start())

    def two_patches(pair, carry):
        one_patch(pair * 2)
        one_patch(pair * 2 + 1)
        return carry

    lax.fori_loop(0, SG // 2, two_patches, 0)

    def finish(g, carry):
        post(g, lambda copy: copy.wait())
        return carry

    lax.fori_loop(0, SG, finish, 0)


def make_patches(plan, pf_index, ints, recv, notes, ratio, beams):
    vmem = pl.BlockSpec(memory_space=pltpu.VMEM)
    smem = pl.BlockSpec(memory_space=pltpu.SMEM)
    return pl.pallas_call(
        subgrid_kernel,
        out_shape=(jax.ShapeDtypeStruct((N_SUB, 128, 256), BF16),) * 2,
        in_specs=[smem] * 3 + [vmem] * 9,
        out_specs=(pl.BlockSpec(memory_space=pl.ANY),) * 2,
        scratch_shapes=[
            pltpu.VMEM((SG * 64 + 1, 8, 128), F32),
            pltpu.VMEM((SG * 64 + 8, 128), F32),
            pltpu.VMEM((SG * 64 + 8, 128), F32),
            pltpu.VMEM((2, N_SUB, 128), F32),
            pltpu.SMEM((SG * LIST + SG,), jnp.int32),
            pltpu.VMEM((SG, 512, 128), F32),
            pltpu.VMEM((SG, 128, 256), BF16),
            pltpu.SemaphoreType.DMA((SG,)),
        ],
        compiler_params=pltpu.CompilerParams(vmem_limit_bytes=48 * MIB),
        name="subgrids",
    )(plan, pf_index, ints, recv, notes, ratio, beams, *dft_tables())


HELPERS = 4
RELAYED = 4
AT_BAD = 8
AT_RELAY = 16
AT_USED = 32
DUMP = 80
AT_ROW = AT_USED + DUMP + 8
AT_COL = AT_ROW + DUMP + 8
PLAN = AT_COL + DUMP + 8
AT_SECOND = N_SUB + HELPERS * RELAYED


def neighbour(tile, k):
    if k < 2:
        return (tile & 28) | ((tile + (1, 3)[k]) & 3)
    return (tile + (4, 28)[k - 2]) & 31


def plan_kernel(me_ref, note_ref, plan_ref, load_scr, mask_scr):
    me = me_ref[0]

    def clear(i, carry):
        for k in range(8):
            plan_ref[i * 8 + k] = 0
        return carry

    def clear_load(i, carry):
        for k in range(8):
            load_scr[i * 8 + k] = 0
        return carry

    lax.fori_loop(0, PLAN // 8, clear, 0)
    lax.fori_loop(0, HELPERS * N_SUB // 8, clear_load, 0)
    for i in range(HELPERS * RELAYED):
        plan_ref[AT_RELAY + i] = -1
    for g in range(SG):
        plan_ref[g] = note_ref[me * 5 + 1, g] >> 1

    def note(entry, used, source, g):
        plan_ref[AT_USED + entry] = used
        plan_ref[AT_ROW + entry] = note_ref[source * 5 + 2, g]
        plan_ref[AT_COL + entry] = note_ref[source * 5 + 3, g] * 128 + note_ref[source * 5 + 4, g]

    def seconds(source):
        mask = jnp.int32(0)
        for g in range(SG):
            mask = mask | (jnp.int32(1) << (note_ref[source * 5 + 1, g] >> 1))
        mask_scr[0] = mask

        def one(g, carry):
            slot = note_ref[source * 5 + 1, g]

            @pl.when((slot & 1) == 1)
            def _():
                tile = slot >> 1
                busy = mask_scr[0]
                best, helper, load = jnp.int32(-1), jnp.int32(0), jnp.int32(RELAYED)
                for k in range(HELPERS):
                    via = neighbour(tile, k)
                    held = load_scr[k * N_SUB + tile]
                    better = (((busy >> via) & 1) == 0) & (held < load)
                    best = jnp.where(better, k, best)
                    helper = jnp.where(better, via, helper)
                    load = jnp.where(better, held, load)

                @pl.when(best >= 0)
                def _():
                    mask_scr[0] = busy | (jnp.int32(1) << helper)
                    load_scr[best * N_SUB + tile] = load + 1
                    place = best * RELAYED + load

                    @pl.when(source == me)
                    def _():
                        plan_ref[g] = helper

                    @pl.when(helper == me)
                    def _():
                        plan_ref[AT_RELAY + place] = source

                    @pl.when(tile == me)
                    def _():
                        note(N_SUB + place, 1, source, g)

                @pl.when(best < 0)
                def _():
                    plan_ref[AT_BAD] = 1

                    @pl.when(source == me)
                    def _():
                        plan_ref[g] = N_SUB + tile

                    @pl.when(tile == me)
                    def _():
                        note(AT_SECOND + source, 1, source, g)

            return carry

        lax.fori_loop(0, SG, one, 0)

    def one_source(source, carry):
        which, any_second = jnp.int32(0), jnp.int32(0)
        for g in range(SG):
            slot = note_ref[source * 5 + 1, g]
            which = jnp.where(slot == 2 * me, g + 1, which)
            any_second = any_second | (slot & 1)
        note(source, jnp.minimum(which, 1), source, jnp.maximum(which - 1, 0))

        @pl.when(any_second > 0)
        def _():
            seconds(source)

        return carry

    lax.fori_loop(0, N_SUB, one_source, 0)


def make_plan(me, ints):
    smem = pl.BlockSpec(memory_space=pltpu.SMEM)
    return pl.pallas_call(
        plan_kernel,
        out_shape=jax.ShapeDtypeStruct((PLAN,), jnp.int32),
        in_specs=[smem] * 2,
        out_specs=smem,
        scratch_shapes=[
            pltpu.SMEM((HELPERS * N_SUB,), jnp.int32),
            pltpu.SMEM((1,), jnp.int32),
        ],
        name="plan",
    )(me, ints)


def relay_kernel(plan_ref, arrived_ref, *outs):
    out_refs, sems = outs[:HELPERS], outs[HELPERS]

    def each(act):
        for k in range(HELPERS):
            for c in range(RELAYED):
                source = plan_ref[AT_RELAY + k * RELAYED + c]

                @pl.when(source >= 0)
                def _(k=k, c=c, source=source):
                    act(
                        pltpu.make_async_copy(
                            arrived_ref.at[source], out_refs[k].at[c], sems.at[k * RELAYED + c]
                        )
                    )

    each(lambda copy: copy.start())
    each(lambda copy: copy.wait())


def relay(plan, arrived):
    hbm = pl.BlockSpec(memory_space=pl.ANY)
    return pl.pallas_call(
        relay_kernel,
        out_shape=(jax.ShapeDtypeStruct((RELAYED, 128, 256), BF16),) * HELPERS,
        in_specs=[pl.BlockSpec(memory_space=pltpu.SMEM), hbm],
        out_specs=(hbm,) * HELPERS,
        scratch_shapes=[pltpu.SemaphoreType.DMA((HELPERS * RELAYED,))],
        name="relay",
    )(plan, arrived)


def deposit_kernel(firsts, plan_ref, *refs):
    recv_refs, out_ref = refs[:-1], refs[-1]
    out_ref[...] = jnp.zeros_like(out_ref)
    tall = SUBPIX + 8
    lane = lax.broadcasted_iota(jnp.int32, (2 * tall, 256), 1)
    blank = jnp.zeros((8, 256), F32)

    for first, recv_ref in zip(firsts, recv_refs):

        def one_slot(slot, carry, first=first, recv_ref=recv_ref):
            @pl.when(plan_ref[AT_USED + first + slot] > 0)
            def _():
                row = plan_ref[AT_ROW + first + slot]
                col = plan_ref[AT_COL + first + slot]
                top = pl.multiple_of(jnp.minimum((row // 8) * 8, BAND - tall), 8)
                start = pl.multiple_of(jnp.minimum((col // 128) * 128, TILE - 256), 128)
                shift = col - start
                patch = recv_ref[slot].astype(F32)
                patch = jnp.concatenate([patch[:SUBPIX], blank, patch[SUBPIX:], blank], 0)
                patch = pltpu.roll(patch, row - top, 0)
                inside = (lane >= shift) & (lane < shift + SUBPIX)
                even = pltpu.roll(patch, shift, 1)
                odd = pltpu.roll(patch, lax.rem(shift + 192, 256), 1)
                for q in range(4):
                    moved = (even, odd)[q & 1]
                    if q >= 2:
                        moved = jnp.concatenate([moved[:, 128:], moved[:, :128]], 1)
                    moved = jnp.where(inside, moved, 0.0)
                    for s in range(2):
                        spot = (0, 2 * q + s, pl.ds(top, tall), pl.ds(start, 256))
                        out_ref[spot] += moved[s * tall : (s + 1) * tall]

            return carry

        lax.fori_loop(0, recv_ref.shape[0], one_slot, 0)


def deposit(plan, firsts, patches):
    vmem = pl.BlockSpec(memory_space=pltpu.VMEM)
    smem = pl.BlockSpec(memory_space=pltpu.SMEM)
    return pl.pallas_call(
        functools.partial(deposit_kernel, firsts),
        out_shape=jax.ShapeDtypeStruct((1, 8, BAND, TILE), F32),
        in_specs=[smem] + [vmem] * len(patches),
        out_specs=vmem,
        compiler_params=pltpu.CompilerParams(vmem_limit_bytes=48 * MIB),
        name="deposit",
    )(plan, *patches)


def shards(
    visibilities,
    row_positions,
    channel_ratio,
    row_subgrid,
    row_count,
    beam_terms,
    subgrid_tile,
    offset_rows,
    offset_cols,
):
    me_sub = lax.axis_index("sub")
    me_pf = lax.axis_index("pf")
    scalars = jnp.concatenate([subgrid_tile[:, 0], offset_rows, offset_cols, row_count])
    send = dispatch(
        scalars, visibilities, row_positions, row_subgrid.reshape(ROWS // 128, 128)
    )
    first = lax.all_to_all(send, "sub", split_axis=0, concat_axis=0, tiled=True)
    recv = jnp.transpose(first[:, :64].reshape(N_SUB, N_PF, 8, 128), (1, 0, 2, 3))
    recv = recv.reshape(N_PF, N_SUB * 8, 128)
    recv = lax.all_to_all(recv, "pf", split_axis=0, concat_axis=0, tiled=True)

    ratio = jnp.repeat(channel_ratio.reshape(8, 8).T.reshape(64), 2)[None, :]
    ints = first[:, 66:71].astype(jnp.int32).reshape(N_SUB * 5, 128)
    plan = make_plan(me_sub.reshape(1), ints)
    bad = plan[AT_BAD] > 0
    patches, second = make_patches(
        plan, me_pf.reshape(1), ints, recv, first, ratio,
        beam_terms.reshape(SG, 2, 8, SUBPIX, SUBPIX),
    )
    arrived = lax.all_to_all(patches, "sub", split_axis=0, concat_axis=0, tiled=True)
    relayed = [
        lax.ppermute(block, "sub", [(neighbour(t, k), t) for t in range(N_SUB)])
        for k, block in enumerate(relay(plan, arrived))
    ]
    firsts = (0,) + tuple(N_SUB + k * RELAYED for k in range(HELPERS))

    def with_second(plan, second, *blocks):
        late = lax.all_to_all(second, "sub", split_axis=0, concat_axis=0, tiled=True)
        return deposit(plan, firsts + (AT_SECOND,), blocks + (late,))

    def without(plan, second, *blocks):
        return deposit(plan, firsts, blocks)

    return lax.cond(bad, with_second, without, plan, second, arrived, *relayed)


def solution(mesh):
    in_specs = (
        P(None, "pf", "sub"),
        P(None, "sub"),
        P(),
        P("sub", None),
        P("sub"),
        P(("sub", "pf"), None, None, None),
        P(("sub", "pf"), None),
        P(("sub", "pf")),
        P(("sub", "pf")),
    )
    out_specs = P(("sub", "pf"), None, None, None)
    return jax.shard_map(shards, mesh=mesh, in_specs=in_specs, out_specs=out_specs, check_vma=False)
```

```python
import functools

import jax
import jax.numpy as jnp
import numpy as np
from jax import lax
from jax.experimental import pallas as pl
from jax.experimental.pallas import tpu as pltpu
from jax.sharding import PartitionSpec as P

SUBPIX = 64
TILE = 2048
BAND = 96
N_SUB = 32
N_PF = 8
SG = 8
ROWS = 2048
F32 = jnp.float32
BF16 = jnp.bfloat16
MIB = 1 << 20
LIST = 80


def fit_even_odd():
    x = np.cos(np.pi * (np.arange(400) + 0.5) / 400) * 0.125 + 0.125
    r = np.sqrt(x)
    cheb = np.polynomial.chebyshev.Chebyshev
    out = []
    for values, degree in ((np.cos(2 * np.pi * r), 7), (np.sin(2 * np.pi * r) / r, 7)):
        poly = cheb.fit(x, values, degree, domain=[0.0, 0.25]).convert(kind=np.polynomial.Polynomial)
        out.append([float(c) for c in poly.coef])
    return out


COS_COEF, SIN_COEF = fit_even_odd()


def horner(coef, x):
    total = jnp.full_like(x, coef[-1])
    for c in coef[-2::-1]:
        total = total * x + c
    return total


def cos_sin_turns(t):
    r = t - jnp.round(t)
    r2 = r * r
    return horner(COS_COEF, r2), horner(SIN_COEF, r2) * r


def split_hi_lo(x):
    hi = x.astype(BF16)
    return hi, (x - hi.astype(F32)).astype(BF16)


def dft_tables():
    centred = np.arange(SUBPIX) - SUBPIX // 2
    angle = -2.0 * np.pi * ((centred[:, None] * centred[None, :]) % SUBPIX) / SUBPIX
    c, s = np.cos(angle), np.sin(angle)
    right = np.block([[c, s], [-s, c]])
    left = np.block([[c, -s], [s, c]]) / SUBPIX

    def parts(m):
        hi = m.astype(np.float32).astype(BF16)
        lo = (m - hi.astype(np.float64)).astype(np.float32).astype(BF16)
        return hi, lo

    rh, rl = parts(right)
    lh, ll = parts(left)
    ramp = np.cos(2 * np.pi * (np.arange(SUBPIX) + 0.5) / SUBPIX)
    window = 0.55 - 0.45 * ramp
    window = (window[:, None] * window[None, :]).astype(np.float32)
    return np.concatenate([rh, rh], 0), rl, np.concatenate([lh, lh], 1), ll, window


def pick_lanes(source, rows):
    row = lax.broadcasted_iota(jnp.int32, (rows, source.shape[1]), 0)
    return jnp.where(row == source, 1.0, 0.0).astype(BF16)


def dispatch_kernel(
    scalar_ref, vis_ref, place_ref, id_ref, send_ref, slot_scr, placed_scr
):
    count = scalar_ref[3 * SG]
    lane = lax.broadcasted_iota(jnp.int32, (128, 128), 1)
    row_in = lax.broadcasted_iota(jnp.int32, (128, 128), 0)
    lane_f = lane.astype(F32)
    for block in range(ROWS // 128):
        ids = jnp.broadcast_to(id_ref[block : block + 1, :].astype(F32), (128, 128)).T

        def seen(chunk, hits):
            return jnp.where(ids == id_ref[pl.ds(chunk, 1), :].astype(F32), 1.0, hits)

        hits = lax.fori_loop(0, block, seen, jnp.zeros((128, 128), F32))
        here = (ids == id_ref[block : block + 1, :].astype(F32)) & (lane < row_in)
        hits = jnp.where(here, 1.0, hits)
        rank = jnp.max(hits, axis=1, keepdims=True)
        slot = jnp.where(row_in + block * 128 < count, ids * 2.0 + rank, -4096.0)
        slot_scr[block * 128 : (block + 1) * 128, :] = slot - lane_f

    note_row = lax.broadcasted_iota(jnp.int32, (16, 128), 0)
    note_lane = lax.broadcasted_iota(jnp.int32, (16, 128), 1)
    notes = jnp.zeros((16, 128), F32)
    tiles_of = [scalar_ref[g] for g in range(SG)]
    for g in range(SG):
        rank = jnp.int32(0)
        for h in range(g):
            rank = rank + (tiles_of[h] == tiles_of[g]).astype(jnp.int32)
        row, col = scalar_ref[SG + g], scalar_ref[2 * SG + g]
        for at, value in enumerate((tiles_of[g] * 2 + rank, row, col >> 7, col & 127)):
            notes = jnp.where((note_row == 3 + at) & (note_lane == g), value.astype(F32), notes)

    order = lax.broadcasted_iota(jnp.int32, (64, 64), 0)
    order = (order & 7) * 8 + (order >> 3)
    order = jnp.where(lax.broadcasted_iota(jnp.int32, (64, 64), 1) == order, 1.0, 0.0).astype(BF16)
    vis = vis_ref[...].astype(F32).reshape(64, ROWS).astype(BF16)
    vis = jnp.dot(order, vis, preferred_element_type=F32)
    place = place_ref[...].astype(F32)
    extra_row = lax.broadcasted_iota(jnp.int32, (16, ROWS), 0)
    extra = jnp.where(extra_row == 2, 1.0, 0.0)
    extra = jnp.where(extra_row == 0, place[0:1], jnp.where(extra_row == 1, place[1:2], extra))
    data = jnp.concatenate([vis, extra], 0).astype(BF16)

    def one_owner(owner, carry):
        rel = slot_scr[...]
        first = (owner * 256).astype(F32)
        picks = jnp.concatenate(
            [
                jnp.where(rel == first, 1.0, 0.0).astype(BF16),
                jnp.where(rel == first + 128.0, 1.0, 0.0).astype(BF16),
            ],
            1,
        )
        placed = jnp.dot(data, picks, preferred_element_type=F32)
        halves = (placed[:, :128], placed[:, 128:])
        for c in range(8):
            both = jnp.concatenate([part[c * 8 : (c + 1) * 8] for part in halves], 0)
            placed_scr[c, pl.ds(pl.multiple_of(owner * 16, 16), 16), :] = both.astype(BF16)
        for k, part in enumerate(halves):
            send_ref[owner * 2 + k, 64:80] = (part[64:80] + notes).astype(BF16)
        return carry

    lax.fori_loop(0, N_SUB // 2, one_owner, 0)

    by_channel = jnp.concatenate([placed_scr[c] for c in range(8)], 1)
    out_lane = lax.broadcasted_iota(jnp.int32, (1, 256), 1)
    for pair in range(N_PF // 2):
        channel, slot = (out_lane >> 4) & 7, out_lane & 15
        source = channel * 128 + (pair * 2 + (out_lane >> 7)) * 16 + slot
        moved = jnp.dot(by_channel, pick_lanes(source, 1024), preferred_element_type=F32)
        for d in range(N_SUB):
            rows = moved[d * 8 : (d + 1) * 8]
            both = jnp.concatenate([rows[:, :128], rows[:, 128:]], 0)
            send_ref[d, pair * 16 : pair * 16 + 16] = both.astype(BF16)


def dispatch(scalars, vis, place, ids):
    vmem = pl.BlockSpec(memory_space=pltpu.VMEM)
    smem = pl.BlockSpec(memory_space=pltpu.SMEM)
    return pl.pallas_call(
        dispatch_kernel,
        out_shape=jax.ShapeDtypeStruct((N_SUB, 80, 128), BF16),
        in_specs=[smem] + [vmem] * 3,
        out_specs=vmem,
        scratch_shapes=[pltpu.VMEM((ROWS, 128), F32), pltpu.VMEM((8, 256, 128), BF16)],
        compiler_params=pltpu.CompilerParams(vmem_limit_bytes=48 * MIB),
        name="dispatch",
    )(scalars, vis, place, ids)


def cmul(a, b):
    return a[0] * b[0] - a[1] * b[1], a[0] * b[1] + a[1] * b[0]


def conj_mul(a, b):
    return a[0] * b[0] + a[1] * b[1], a[0] * b[1] - a[1] * b[0]


def cadd(a, b):
    return a[0] + b[0], a[1] + b[1]


def corrected_image(image, left, right, window):
    middle = {}
    for i in range(2):
        for j in range(2):
            middle[i, j] = cadd(conj_mul(left[i], image[j]), conj_mul(left[2 + i], image[2 + j]))
    out = []
    for i in range(2):
        for j in range(2):
            re, im = cadd(cmul(middle[i, 0], right[j]), cmul(middle[i, 1], right[2 + j]))
            out.append((re * window, im * window))
    return out


def phases(base_turns, tile_turns):
    cb, sb = cos_sin_turns(base_turns)
    ca, sa = cos_sin_turns(tile_turns)
    cos_out, sin_out = [], []
    for a in range(8):
        c, s = ca[a : a + 1], sa[a : a + 1]
        cos_out.append(cb * c - sb * s)
        sin_out.append(cb * s + sb * c)
    return jnp.concatenate(cos_out, 0), jnp.concatenate(sin_out, 0)


def subgrid_kernel(
    plan_ref, pf_ref, note_ref, recv_ref, notes_ref, ratio_ref, beam_ref, rt2_ref, rtl_ref, lt2_ref, ltl_ref,
    window_ref, send_ref, send2_ref, vis_scr, u_scr, v_scr, place_scr, list_scr, total_scr, patch_scr, sems,
):
    tile_lane = lax.broadcasted_iota(jnp.int32, (8, 128), 1)
    odd = (tile_lane & 1) == 1
    base = pf_ref[0] * 16

    def read_place(source, carry):
        place = notes_ref[source, 64:80].astype(F32)
        place_scr[0, pl.ds(source, 1)] = place[0:1]
        place_scr[1, pl.ds(source, 1)] = place[1:2]
        return carry

    lax.fori_loop(0, N_SUB, read_place, 0)

    by_sender = jnp.concatenate([recv_ref[p] for p in range(N_PF)], 1)
    out_lane = lax.broadcasted_iota(jnp.int32, (1, 256), 1)
    from_lane = ((out_lane >> 1) & 7) * 128 + ((out_lane >> 4) & 7) * 16 + (out_lane >> 7)

    def regroup(g, carry):
        picks = pick_lanes(from_lane + g * 2, 1024)
        moved = jnp.dot(by_sender, picks, preferred_element_type=F32)
        for j in range(2):
            block = moved[:, j * 128 : (j + 1) * 128].reshape(N_SUB, 8, 128)
            vis_scr[pl.ds(g * 64 + j * 32, N_SUB)] = block
        count = jnp.int32(0)
        for j in range(2):
            for source in range(N_SUB):
                list_scr[g * LIST + count] = g * 64 + (j * 32 + source)
                count = count + note_ref[source * 8 + 2, base + g * 2 + j]
        for k in range(16):
            list_scr[g * LIST + count + k] = 512
        list_scr[SG * LIST + g] = count
        return carry

    lax.fori_loop(0, SG, regroup, 0)
    vis_scr[512] = jnp.zeros((8, 128), F32)

    ratio = ratio_ref[...]
    for part, scr in ((0, u_scr), (1, v_scr)):
        mine = pltpu.roll(place_scr[part], lax.rem(128 - base, 128), 1)
        for g in range(SG):
            for j in range(2):
                k = g * 2 + j
                scr[g * 64 + j * 32 : g * 64 + j * 32 + 32, :] = mine[:, k : k + 1] * ratio
        scr[512:520, :] = jnp.zeros((8, 128), F32)

    units = 8
    eight = lax.broadcasted_iota(jnp.int32, (8, 128 * units), 0).astype(F32)
    base_x = eight * (1.0 / 64.0)
    tile_x = (eight - 4.0) * (1.0 / 8.0)
    half_lane = lax.broadcasted_iota(jnp.int32, (SUBPIX, 128), 1) < SUBPIX
    window = window_ref[...]

    def post(g, act):
        slot = plan_ref[g]

        @pl.when(slot < N_SUB)
        def _():
            act(pltpu.make_async_copy(patch_scr.at[g], send_ref.at[slot], sems.at[g]))

        @pl.when(slot >= N_SUB)
        def _():
            act(pltpu.make_async_copy(patch_scr.at[g], send2_ref.at[slot - N_SUB], sems.at[g]))

    def one_subgrid(g, carry):
        def accumulate(step, inner):
            first = g * LIST + step * (2 * units)
            picked = [list_scr[first + k] for k in range(2 * units)]

            def lanes(load, mask):
                return jnp.concatenate(
                    [
                        jnp.where(mask, load(picked[2 * k + 1]), load(picked[2 * k]))
                        for k in range(units)
                    ],
                    1,
                )

            u = lanes(lambda i: u_scr[pl.ds(i, 1), :], odd[0:1])
            v = lanes(lambda i: v_scr[pl.ds(i, 1), :], odd[0:1])
            vis = lanes(lambda i: vis_scr[i], odd)
            cos_u, sin_u = phases(u * base_x, u * tile_x)
            cos_v, sin_v = phases(v * base_x, v * tile_x)
            rows = []
            for q in range(4):
                re, im = vis[2 * q : 2 * q + 1], vis[2 * q + 1 : 2 * q + 2]
                rows.append((re * cos_u - im * sin_u).astype(BF16))
                rows.append((re * sin_u + im * cos_u).astype(BF16))
            left = jnp.concatenate(rows, 0)
            right = jnp.concatenate([cos_v.astype(BF16), sin_v.astype(BF16)], 0)
            total_scr[g] += lax.dot_general(
                left, right, (((1,), (1,)), ((), ())), preferred_element_type=F32
            )
            return inner

        steps = (list_scr[SG * LIST + g] + (2 * units - 1)) // (2 * units)
        total_scr[g] = jnp.zeros((512, 128), F32)
        lax.fori_loop(0, steps, accumulate, 0)
        return carry

    lax.fori_loop(0, SG, one_subgrid, 0)

    def one_patch(g):
        total = total_scr[g]
        image = []
        for q in range(4):
            re = total[q * 128 : q * 128 + 64]
            im = total[q * 128 + 64 : q * 128 + 128]
            image.append((re[:, :64] - im[:, 64:], re[:, 64:] + im[:, :64]))
        beams = [
            [
                (beam_ref[g, side, 2 * e].astype(F32), beam_ref[g, side, 2 * e + 1].astype(F32))
                for e in range(4)
            ]
            for side in range(2)
        ]
        pieces = corrected_image(image, beams[0], beams[1], window)
        stacked = jnp.concatenate([jnp.concatenate([re, im], 1) for re, im in pieces], 0)
        hi, lo = split_hi_lo(stacked)
        mid = jnp.dot(jnp.concatenate([hi, lo], 1), rt2_ref[...], preferred_element_type=F32)
        mid = mid + jnp.dot(hi, rtl_ref[...], preferred_element_type=F32)
        mids = [mid[q * 64 : (q + 1) * 64] for q in range(4)]
        upper, lower = [], []
        for q in (0, 2):
            upper.append(jnp.where(half_lane, mids[q], pltpu.roll(mids[q + 1], 64, 1)))
            lower.append(jnp.where(half_lane, pltpu.roll(mids[q], 64, 1), mids[q + 1]))
        both = jnp.concatenate([jnp.concatenate(upper, 1), jnp.concatenate(lower, 1)], 0)
        hi, lo = split_hi_lo(both)
        out = jnp.dot(lt2_ref[...], jnp.concatenate([hi, lo], 0), preferred_element_type=F32)
        out = out + jnp.dot(ltl_ref[...], hi, preferred_element_type=F32)
        patch_scr[g] = out.astype(BF16)
        post(g, lambda copy: copy.start())

    def two_patches(pair, carry):
        one_patch(pair * 2)
        one_patch(pair * 2 + 1)
        return carry

    lax.fori_loop(0, SG // 2, two_patches, 0)

    def finish(g, carry):
        post(g, lambda copy: copy.wait())
        return carry

    lax.fori_loop(0, SG, finish, 0)


def make_patches(plan, pf_index, ints, recv, notes, ratio, beams):
    vmem = pl.BlockSpec(memory_space=pltpu.VMEM)
    smem = pl.BlockSpec(memory_space=pltpu.SMEM)
    return pl.pallas_call(
        subgrid_kernel,
        out_shape=(jax.ShapeDtypeStruct((N_SUB, 128, 256), BF16),) * 2,
        in_specs=[smem] * 3 + [vmem] * 9,
        out_specs=(pl.BlockSpec(memory_space=pl.ANY),) * 2,
        scratch_shapes=[
            pltpu.VMEM((SG * 64 + 1, 8, 128), F32),
            pltpu.VMEM((SG * 64 + 8, 128), F32),
            pltpu.VMEM((SG * 64 + 8, 128), F32),
            pltpu.VMEM((2, N_SUB, 128), F32),
            pltpu.SMEM((SG * LIST + SG,), jnp.int32),
            pltpu.VMEM((SG, 512, 128), F32),
            pltpu.VMEM((SG, 128, 256), BF16),
            pltpu.SemaphoreType.DMA((SG,)),
        ],
        compiler_params=pltpu.CompilerParams(vmem_limit_bytes=48 * MIB),
        name="subgrids",
    )(plan, pf_index, ints, recv, notes, ratio, beams, *dft_tables())


HELPERS = 4
RELAYED = 4
TOGETHER = 4
AT_BAD = 8
AT_RELAY = 16
AT_USED = 32
DUMP = 80
AT_ROW = AT_USED + DUMP + 8
AT_COL = AT_ROW + DUMP + 8
PLAN = AT_COL + DUMP + 8
AT_SECOND = N_SUB + HELPERS * RELAYED


def neighbour(tile, k):
    if k < 2:
        return (tile & 28) | ((tile + (1, 3)[k]) & 3)
    return (tile + (4, 28)[k - 2]) & 31


def plan_kernel(me_ref, note_ref, plan_ref, load_scr, mask_scr):
    me = me_ref[0]

    def clear(i, carry):
        for k in range(8):
            plan_ref[i * 8 + k] = 0
        return carry

    def clear_load(i, carry):
        for k in range(8):
            load_scr[i * 8 + k] = 0
        return carry

    lax.fori_loop(0, PLAN // 8, clear, 0)
    lax.fori_loop(0, HELPERS * N_SUB // 8, clear_load, 0)
    for i in range(HELPERS * RELAYED):
        plan_ref[AT_RELAY + i] = -1
    for g in range(SG):
        plan_ref[g] = note_ref[me * 8 + 3, g] >> 1

    def note(entry, used, source, g):
        plan_ref[AT_USED + entry] = used
        plan_ref[AT_ROW + entry] = note_ref[source * 8 + 4, g]
        plan_ref[AT_COL + entry] = note_ref[source * 8 + 5, g] * 128 + note_ref[source * 8 + 6, g]

    def seconds(source):
        mask = jnp.int32(0)
        for g in range(SG):
            mask = mask | (jnp.int32(1) << (note_ref[source * 8 + 3, g] >> 1))
        mask_scr[0] = mask

        def one(g, carry):
            slot = note_ref[source * 8 + 3, g]

            @pl.when((slot & 1) == 1)
            def _():
                tile = slot >> 1
                busy = mask_scr[0]
                best, helper, load = jnp.int32(-1), jnp.int32(0), jnp.int32(RELAYED)
                for k in range(HELPERS):
                    via = neighbour(tile, k)
                    held = load_scr[k * N_SUB + tile]
                    better = (((busy >> via) & 1) == 0) & (held < load)
                    best = jnp.where(better, k, best)
                    helper = jnp.where(better, via, helper)
                    load = jnp.where(better, held, load)

                @pl.when(best >= 0)
                def _():
                    mask_scr[0] = busy | (jnp.int32(1) << helper)
                    load_scr[best * N_SUB + tile] = load + 1
                    place = best * RELAYED + load

                    @pl.when(source == me)
                    def _():
                        plan_ref[g] = helper

                    @pl.when(helper == me)
                    def _():
                        plan_ref[AT_RELAY + place] = source

                    @pl.when(tile == me)
                    def _():
                        note(N_SUB + place, 1, source, g)

                @pl.when(best < 0)
                def _():
                    plan_ref[AT_BAD] = 1

                    @pl.when(source == me)
                    def _():
                        plan_ref[g] = N_SUB + tile

                    @pl.when(tile == me)
                    def _():
                        note(AT_SECOND + source, 1, source, g)

            return carry

        lax.fori_loop(0, SG, one, 0)

    def one_source(source, carry):
        which, any_second = jnp.int32(0), jnp.int32(0)
        for g in range(SG):
            slot = note_ref[source * 8 + 3, g]
            which = jnp.where(slot == 2 * me, g + 1, which)
            any_second = any_second | (slot & 1)
        note(source, jnp.minimum(which, 1), source, jnp.maximum(which - 1, 0))

        @pl.when(any_second > 0)
        def _():
            seconds(source)

        return carry

    lax.fori_loop(0, N_SUB, one_source, 0)


def make_plan(me, ints):
    smem = pl.BlockSpec(memory_space=pltpu.SMEM)
    return pl.pallas_call(
        plan_kernel,
        out_shape=jax.ShapeDtypeStruct((PLAN,), jnp.int32),
        in_specs=[smem] * 2,
        out_specs=smem,
        scratch_shapes=[
            pltpu.SMEM((HELPERS * N_SUB,), jnp.int32),
            pltpu.SMEM((1,), jnp.int32),
        ],
        name="plan",
    )(me, ints)


def relay_kernel(plan_ref, arrived_ref, *outs):
    out_refs, sems = outs[:HELPERS], outs[HELPERS]

    def each(act):
        for k in range(HELPERS):
            for c in range(RELAYED):
                source = plan_ref[AT_RELAY + k * RELAYED + c]

                @pl.when(source >= 0)
                def _(k=k, c=c, source=source):
                    act(
                        pltpu.make_async_copy(
                            arrived_ref.at[source], out_refs[k].at[c], sems.at[k * RELAYED + c]
                        )
                    )

    each(lambda copy: copy.start())
    each(lambda copy: copy.wait())


def relay(plan, arrived):
    hbm = pl.BlockSpec(memory_space=pl.ANY)
    return pl.pallas_call(
        relay_kernel,
        out_shape=(jax.ShapeDtypeStruct((RELAYED, 128, 256), BF16),) * HELPERS,
        in_specs=[pl.BlockSpec(memory_space=pltpu.SMEM), hbm],
        out_specs=(hbm,) * HELPERS,
        scratch_shapes=[pltpu.SemaphoreType.DMA((HELPERS * RELAYED,))],
        name="relay",
    )(plan, arrived)


def deposit_kernel(firsts, plan_ref, *refs):
    recv_refs, out_ref, list_scr = refs[:-2], refs[-2], refs[-1]
    out_ref[...] = jnp.zeros_like(out_ref)
    tall = SUBPIX + 8
    lane = lax.broadcasted_iota(jnp.int32, (2 * tall, 256), 1)
    blank = jnp.zeros((8, 256), F32)

    def placed(entry, recv_ref, slot, real):
        row = jnp.where(real, plan_ref[AT_ROW + entry], 0)
        col = jnp.where(real, plan_ref[AT_COL + entry], 0)
        top = pl.multiple_of(jnp.minimum((row // 8) * 8, BAND - tall), 8)
        start = pl.multiple_of(jnp.minimum((col // 128) * 128, TILE - 256), 128)
        shift = col - start
        patch = recv_ref[slot].astype(F32)
        patch = jnp.concatenate([patch[:SUBPIX], blank, patch[SUBPIX:], blank], 0)
        patch = pltpu.roll(patch, row - top, 0)
        inside = (lane >= shift) & (lane < jnp.where(real, shift + SUBPIX, shift))
        even = pltpu.roll(patch, shift, 1)
        odd = pltpu.roll(patch, lax.rem(shift + 192, 256), 1)
        parts = []
        for q in range(4):
            moved = (even, odd)[q & 1]
            if q >= 2:
                moved = jnp.concatenate([moved[:, 128:], moved[:, :128]], 1)
            parts.append(jnp.where(inside, moved, 0.0))
        return parts, top, start

    def add(parts, top, start):
        for q in range(4):
            for s in range(2):
                spot = (0, 2 * q + s, pl.ds(top, tall), pl.ds(start, 256))
                out_ref[spot] += parts[q][s * tall : (s + 1) * tall]

    def add_listed(first, recv_ref):
        def collect(slot, count):
            list_scr[count] = slot
            return count + plan_ref[AT_USED + first + slot]

        count = lax.fori_loop(0, N_SUB, collect, jnp.int32(0))
        for k in range(TOGETHER):
            list_scr[count + k] = 0

        def some(step, carry):
            ready = []
            for k in range(TOGETHER):
                at = step * TOGETHER + k
                slot = list_scr[at]
                ready.append(placed(first + slot, recv_ref, slot, at < count))
            for one in ready:
                add(*one)
            return carry

        lax.fori_loop(0, (count + TOGETHER - 1) // TOGETHER, some, 0)

    add_listed(firsts[0], recv_refs[0])

    def relayed(slot, carry):
        reals = [plan_ref[AT_USED + first + slot] for first in firsts[1 : 1 + HELPERS]]

        @pl.when(sum(reals) > 0)
        def _():
            ready = [
                placed(first + slot, recv_ref, slot, real > 0)
                for first, recv_ref, real in zip(firsts[1:], recv_refs[1:], reals)
            ]
            for one in ready:
                add(*one)

        return carry

    lax.fori_loop(0, RELAYED, relayed, 0)
    for first, recv_ref in zip(firsts[1 + HELPERS :], recv_refs[1 + HELPERS :]):
        add_listed(first, recv_ref)


def deposit(plan, firsts, patches):
    vmem = pl.BlockSpec(memory_space=pltpu.VMEM)
    smem = pl.BlockSpec(memory_space=pltpu.SMEM)
    return pl.pallas_call(
        functools.partial(deposit_kernel, firsts),
        out_shape=jax.ShapeDtypeStruct((1, 8, BAND, TILE), F32),
        in_specs=[smem] + [vmem] * len(patches),
        out_specs=vmem,
        scratch_shapes=[pltpu.SMEM((N_SUB + TOGETHER,), jnp.int32)],
        compiler_params=pltpu.CompilerParams(vmem_limit_bytes=48 * MIB),
        name="deposit",
    )(plan, *patches)


def shards(
    visibilities,
    row_positions,
    channel_ratio,
    row_subgrid,
    row_count,
    beam_terms,
    subgrid_tile,
    offset_rows,
    offset_cols,
):
    me_sub = lax.axis_index("sub")
    me_pf = lax.axis_index("pf")
    scalars = jnp.concatenate([subgrid_tile[:, 0], offset_rows, offset_cols, row_count])
    send = dispatch(
        scalars, visibilities, row_positions, row_subgrid.reshape(ROWS // 128, 128)
    )
    first = lax.all_to_all(send, "sub", split_axis=0, concat_axis=0, tiled=True)
    recv = jnp.transpose(first[:, :64].reshape(N_SUB, N_PF, 8, 128), (1, 0, 2, 3))
    recv = recv.reshape(N_PF, N_SUB * 8, 128)
    recv = lax.all_to_all(recv, "pf", split_axis=0, concat_axis=0, tiled=True)

    ratio = jnp.repeat(channel_ratio.reshape(8, 8).T.reshape(64), 2)[None, :]
    ints = first[:, 64:72].astype(jnp.int32).reshape(N_SUB * 8, 128)
    plan = make_plan(me_sub.reshape(1), ints)
    bad = plan[AT_BAD] > 0
    patches, second = make_patches(
        plan, me_pf.reshape(1), ints, recv, first, ratio,
        beam_terms.reshape(SG, 2, 8, SUBPIX, SUBPIX),
    )
    arrived = lax.all_to_all(patches, "sub", split_axis=0, concat_axis=0, tiled=True)
    relayed = [
        lax.ppermute(block, "sub", [(neighbour(t, k), t) for t in range(N_SUB)])
        for k, block in enumerate(relay(plan, arrived))
    ]
    firsts = (0,) + tuple(N_SUB + k * RELAYED for k in range(HELPERS))

    def with_second(plan, second, *blocks):
        late = lax.all_to_all(second, "sub", split_axis=0, concat_axis=0, tiled=True)
        return deposit(plan, firsts + (AT_SECOND,), blocks + (late,))

    def without(plan, second, *blocks):
        return deposit(plan, firsts, blocks)

    return lax.cond(bad, with_second, without, plan, second, arrived, *relayed)


def solution(mesh):
    in_specs = (
        P(None, "pf", "sub"),
        P(None, "sub"),
        P(),
        P("sub", None),
        P("sub"),
        P(("sub", "pf"), None, None, None),
        P(("sub", "pf"), None),
        P(("sub", "pf")),
        P(("sub", "pf")),
    )
    out_specs = P(("sub", "pf"), None, None, None)
    return jax.shard_map(shards, mesh=mesh, in_specs=in_specs, out_specs=out_specs, check_vma=False)
```

```python
import functools

import jax
import jax.numpy as jnp
import numpy as np
from jax import lax
from jax.experimental import pallas as pl
from jax.experimental.pallas import tpu as pltpu
from jax.sharding import PartitionSpec as P

SUBPIX = 64
TILE = 2048
BAND = 96
N_SUB = 32
N_PF = 8
SG = 8
ROWS = 2048
F32 = jnp.float32
BF16 = jnp.bfloat16
MIB = 1 << 20
LIST = 80


def fit_even_odd():
    x = np.cos(np.pi * (np.arange(400) + 0.5) / 400) * 0.125 + 0.125
    r = np.sqrt(x)
    cheb = np.polynomial.chebyshev.Chebyshev
    out = []
    for values, degree in ((np.cos(2 * np.pi * r), 7), (np.sin(2 * np.pi * r) / r, 7)):
        poly = cheb.fit(x, values, degree, domain=[0.0, 0.25]).convert(kind=np.polynomial.Polynomial)
        out.append([float(c) for c in poly.coef])
    return out


COS_COEF, SIN_COEF = fit_even_odd()


def horner(coef, x):
    total = jnp.full_like(x, coef[-1])
    for c in coef[-2::-1]:
        total = total * x + c
    return total


def cos_sin_turns(t):
    r = t - jnp.round(t)
    r2 = r * r
    return horner(COS_COEF, r2), horner(SIN_COEF, r2) * r


def split_hi_lo(x):
    hi = x.astype(BF16)
    return hi, (x - hi.astype(F32)).astype(BF16)


def dft_tables():
    centred = np.arange(SUBPIX) - SUBPIX // 2
    angle = -2.0 * np.pi * ((centred[:, None] * centred[None, :]) % SUBPIX) / SUBPIX
    c, s = np.cos(angle), np.sin(angle)
    right = np.block([[c, s], [-s, c]])
    left = np.block([[c, -s], [s, c]]) / SUBPIX

    def parts(m):
        hi = m.astype(np.float32).astype(BF16)
        lo = (m - hi.astype(np.float64)).astype(np.float32).astype(BF16)
        return hi, lo

    rh, rl = parts(right)
    lh, ll = parts(left)
    ramp = np.cos(2 * np.pi * (np.arange(SUBPIX) + 0.5) / SUBPIX)
    window = 0.55 - 0.45 * ramp
    window = (window[:, None] * window[None, :]).astype(np.float32)
    return np.concatenate([rh, rh], 0), rl, np.concatenate([lh, lh], 1), ll, window


def pick_lanes(source, rows):
    row = lax.broadcasted_iota(jnp.int32, (rows, source.shape[1]), 0)
    return jnp.where(row == source, 1.0, 0.0).astype(BF16)


def dispatch_kernel(
    scalar_ref, vis_ref, place_ref, id_ref, send_ref, slot_scr, placed_scr
):
    count = scalar_ref[3 * SG]
    lane = lax.broadcasted_iota(jnp.int32, (128, 128), 1)
    row_in = lax.broadcasted_iota(jnp.int32, (128, 128), 0)
    lane_f = lane.astype(F32)
    for block in range(ROWS // 128):
        ids = jnp.broadcast_to(id_ref[block : block + 1, :].astype(F32), (128, 128)).T

        def seen(chunk, hits):
            return jnp.where(ids == id_ref[pl.ds(chunk, 1), :].astype(F32), 1.0, hits)

        hits = lax.fori_loop(0, block, seen, jnp.zeros((128, 128), F32))
        here = (ids == id_ref[block : block + 1, :].astype(F32)) & (lane < row_in)
        hits = jnp.where(here, 1.0, hits)
        rank = jnp.max(hits, axis=1, keepdims=True)
        slot = jnp.where(row_in + block * 128 < count, ids * 2.0 + rank, -4096.0)
        slot_scr[block * 128 : (block + 1) * 128, :] = slot - lane_f

    note_row = lax.broadcasted_iota(jnp.int32, (16, 128), 0)
    note_lane = lax.broadcasted_iota(jnp.int32, (16, 128), 1)
    notes = jnp.zeros((16, 128), F32)
    tiles_of = [scalar_ref[g] for g in range(SG)]
    for g in range(SG):
        rank = jnp.int32(0)
        for h in range(g):
            rank = rank + (tiles_of[h] == tiles_of[g]).astype(jnp.int32)
        row, col = scalar_ref[SG + g], scalar_ref[2 * SG + g]
        for at, value in enumerate((tiles_of[g] * 2 + rank, row, col >> 7, col & 127)):
            notes = jnp.where((note_row == 3 + at) & (note_lane == g), value.astype(F32), notes)

    order = lax.broadcasted_iota(jnp.int32, (64, 64), 0)
    order = (order & 7) * 8 + (order >> 3)
    order = jnp.where(lax.broadcasted_iota(jnp.int32, (64, 64), 1) == order, 1.0, 0.0).astype(BF16)
    vis = vis_ref[...].astype(F32).reshape(64, ROWS).astype(BF16)
    vis = jnp.dot(order, vis, preferred_element_type=F32)
    place = place_ref[...].astype(F32)
    extra_row = lax.broadcasted_iota(jnp.int32, (16, ROWS), 0)
    extra = jnp.where(extra_row == 2, 1.0, 0.0)
    extra = jnp.where(extra_row == 0, place[0:1], jnp.where(extra_row == 1, place[1:2], extra))
    data = jnp.concatenate([vis, extra], 0).astype(BF16)

    def one_owner(owner, carry):
        rel = slot_scr[...]
        first = (owner * 256).astype(F32)
        picks = jnp.concatenate(
            [
                jnp.where(rel == first, 1.0, 0.0).astype(BF16),
                jnp.where(rel == first + 128.0, 1.0, 0.0).astype(BF16),
            ],
            1,
        )
        placed = jnp.dot(data, picks, preferred_element_type=F32)
        halves = (placed[:, :128], placed[:, 128:])
        for c in range(8):
            both = jnp.concatenate([part[c * 8 : (c + 1) * 8] for part in halves], 0)
            placed_scr[c, pl.ds(pl.multiple_of(owner * 16, 16), 16), :] = both.astype(BF16)
        for k, part in enumerate(halves):
            send_ref[owner * 2 + k, 64:80] = (part[64:80] + notes).astype(BF16)
        return carry

    lax.fori_loop(0, N_SUB // 2, one_owner, 0)

    by_channel = jnp.concatenate([placed_scr[c] for c in range(8)], 1)
    out_lane = lax.broadcasted_iota(jnp.int32, (1, 256), 1)
    for pair in range(N_PF // 2):
        channel, slot = (out_lane >> 4) & 7, out_lane & 15
        source = channel * 128 + (pair * 2 + (out_lane >> 7)) * 16 + slot
        moved = jnp.dot(by_channel, pick_lanes(source, 1024), preferred_element_type=F32)
        for d in range(N_SUB):
            rows = moved[d * 8 : (d + 1) * 8]
            both = jnp.concatenate([rows[:, :128], rows[:, 128:]], 0)
            send_ref[d, pair * 16 : pair * 16 + 16] = both.astype(BF16)


def dispatch(scalars, vis, place, ids):
    vmem = pl.BlockSpec(memory_space=pltpu.VMEM)
    smem = pl.BlockSpec(memory_space=pltpu.SMEM)
    return pl.pallas_call(
        dispatch_kernel,
        out_shape=jax.ShapeDtypeStruct((N_SUB, 80, 128), BF16),
        in_specs=[smem] + [vmem] * 3,
        out_specs=vmem,
        scratch_shapes=[pltpu.VMEM((ROWS, 128), F32), pltpu.VMEM((8, 256, 128), BF16)],
        compiler_params=pltpu.CompilerParams(vmem_limit_bytes=48 * MIB),
        name="dispatch",
    )(scalars, vis, place, ids)


def cmul(a, b):
    return a[0] * b[0] - a[1] * b[1], a[0] * b[1] + a[1] * b[0]


def conj_mul(a, b):
    return a[0] * b[0] + a[1] * b[1], a[0] * b[1] - a[1] * b[0]


def cadd(a, b):
    return a[0] + b[0], a[1] + b[1]


def corrected_image(image, left, right, window):
    middle = {}
    for i in range(2):
        for j in range(2):
            middle[i, j] = cadd(conj_mul(left[i], image[j]), conj_mul(left[2 + i], image[2 + j]))
    out = []
    for i in range(2):
        for j in range(2):
            re, im = cadd(cmul(middle[i, 0], right[j]), cmul(middle[i, 1], right[2 + j]))
            out.append((re * window, im * window))
    return out


def phases(base_turns, tile_turns):
    cb, sb = cos_sin_turns(base_turns)
    ca, sa = cos_sin_turns(tile_turns)
    cos_out, sin_out = [], []
    for a in range(8):
        c, s = ca[a : a + 1], sa[a : a + 1]
        cos_out.append(cb * c - sb * s)
        sin_out.append(cb * s + sb * c)
    return jnp.concatenate(cos_out, 0), jnp.concatenate(sin_out, 0)


def subgrid_kernel(
    plan_ref, pf_ref, note_ref, recv_ref, notes_ref, ratio_ref, beam_ref, rt2_ref, rtl_ref, lt2_ref, ltl_ref,
    window_ref, send_ref, send2_ref, vis_scr, u_scr, v_scr, place_scr, list_scr, total_scr, patch_scr, sems,
):
    tile_lane = lax.broadcasted_iota(jnp.int32, (8, 128), 1)
    odd = (tile_lane & 1) == 1
    base = pf_ref[0] * 16

    def read_place(source, carry):
        place = notes_ref[source, 64:80].astype(F32)
        place_scr[0, pl.ds(source, 1)] = place[0:1]
        place_scr[1, pl.ds(source, 1)] = place[1:2]
        return carry

    lax.fori_loop(0, N_SUB, read_place, 0)

    by_sender = jnp.concatenate([recv_ref[p] for p in range(N_PF)], 1)
    out_lane = lax.broadcasted_iota(jnp.int32, (1, 256), 1)
    from_lane = ((out_lane >> 1) & 7) * 128 + ((out_lane >> 4) & 7) * 16 + (out_lane >> 7)

    def regroup(g, carry):
        picks = pick_lanes(from_lane + g * 2, 1024)
        moved = jnp.dot(by_sender, picks, preferred_element_type=F32)
        for j in range(2):
            block = moved[:, j * 128 : (j + 1) * 128].reshape(N_SUB, 8, 128)
            vis_scr[pl.ds(g * 64 + j * 32, N_SUB)] = block
        count = jnp.int32(0)
        for j in range(2):
            for source in range(N_SUB):
                list_scr[g * LIST + count] = g * 64 + (j * 32 + source)
                count = count + note_ref[source * 8 + 2, base + g * 2 + j]
        for k in range(16):
            list_scr[g * LIST + count + k] = 512
        list_scr[SG * LIST + g] = count
        return carry

    lax.fori_loop(0, SG, regroup, 0)
    vis_scr[512] = jnp.zeros((8, 128), F32)

    ratio = ratio_ref[...]
    for part, scr in ((0, u_scr), (1, v_scr)):
        mine = pltpu.roll(place_scr[part], lax.rem(128 - base, 128), 1)
        for g in range(SG):
            for j in range(2):
                k = g * 2 + j
                scr[g * 64 + j * 32 : g * 64 + j * 32 + 32, :] = mine[:, k : k + 1] * ratio
        scr[512:520, :] = jnp.zeros((8, 128), F32)

    units = 8
    eight = lax.broadcasted_iota(jnp.int32, (8, 128 * units), 0).astype(F32)
    base_x = eight * (1.0 / 64.0)
    tile_x = (eight - 4.0) * (1.0 / 8.0)
    half_lane = lax.broadcasted_iota(jnp.int32, (SUBPIX, 128), 1) < SUBPIX
    window = window_ref[...]

    def post(g, act):
        slot = plan_ref[g]

        @pl.when(slot < N_SUB)
        def _():
            act(pltpu.make_async_copy(patch_scr.at[g], send_ref.at[slot], sems.at[g]))

        @pl.when(slot >= N_SUB)
        def _():
            act(pltpu.make_async_copy(patch_scr.at[g], send2_ref.at[slot - N_SUB], sems.at[g]))

    def one_subgrid(g, carry):
        def accumulate(step, inner):
            first = g * LIST + step * (2 * units)
            picked = [list_scr[first + k] for k in range(2 * units)]

            def lanes(load, mask):
                return jnp.concatenate(
                    [
                        jnp.where(mask, load(picked[2 * k + 1]), load(picked[2 * k]))
                        for k in range(units)
                    ],
                    1,
                )

            u = lanes(lambda i: u_scr[pl.ds(i, 1), :], odd[0:1])
            v = lanes(lambda i: v_scr[pl.ds(i, 1), :], odd[0:1])
            vis = lanes(lambda i: vis_scr[i], odd)
            cos_u, sin_u = phases(u * base_x, u * tile_x)
            cos_v, sin_v = phases(v * base_x, v * tile_x)
            rows = []
            for q in range(4):
                re, im = vis[2 * q : 2 * q + 1], vis[2 * q + 1 : 2 * q + 2]
                rows.append((re * cos_u - im * sin_u).astype(BF16))
                rows.append((re * sin_u + im * cos_u).astype(BF16))
            left = jnp.concatenate(rows, 0)
            right = jnp.concatenate([cos_v.astype(BF16), sin_v.astype(BF16)], 0)
            total_scr[g] += lax.dot_general(
                left, right, (((1,), (1,)), ((), ())), preferred_element_type=F32
            )
            return inner

        steps = (list_scr[SG * LIST + g] + (2 * units - 1)) // (2 * units)
        total_scr[g] = jnp.zeros((512, 128), F32)
        lax.fori_loop(0, steps, accumulate, 0)
        return carry

    lax.fori_loop(0, SG, one_subgrid, 0)

    def one_patch(g):
        total = total_scr[g]
        image = []
        for q in range(4):
            re = total[q * 128 : q * 128 + 64]
            im = total[q * 128 + 64 : q * 128 + 128]
            image.append((re[:, :64] - im[:, 64:], re[:, 64:] + im[:, :64]))
        beams = [
            [
                (beam_ref[g, side, 2 * e].astype(F32), beam_ref[g, side, 2 * e + 1].astype(F32))
                for e in range(4)
            ]
            for side in range(2)
        ]
        pieces = corrected_image(image, beams[0], beams[1], window)
        stacked = jnp.concatenate([jnp.concatenate([re, im], 1) for re, im in pieces], 0)
        hi, lo = split_hi_lo(stacked)
        mid = jnp.dot(jnp.concatenate([hi, lo], 1), rt2_ref[...], preferred_element_type=F32)
        mid = mid + jnp.dot(hi, rtl_ref[...], preferred_element_type=F32)
        mids = [mid[q * 64 : (q + 1) * 64] for q in range(4)]
        upper, lower = [], []
        for q in (0, 2):
            upper.append(jnp.where(half_lane, mids[q], pltpu.roll(mids[q + 1], 64, 1)))
            lower.append(jnp.where(half_lane, pltpu.roll(mids[q], 64, 1), mids[q + 1]))
        both = jnp.concatenate([jnp.concatenate(upper, 1), jnp.concatenate(lower, 1)], 0)
        hi, lo = split_hi_lo(both)
        out = jnp.dot(lt2_ref[...], jnp.concatenate([hi, lo], 0), preferred_element_type=F32)
        out = out + jnp.dot(ltl_ref[...], hi, preferred_element_type=F32)
        patch_scr[g] = out.astype(BF16)
        post(g, lambda copy: copy.start())

    def two_patches(pair, carry):
        one_patch(pair * 2)
        one_patch(pair * 2 + 1)
        return carry

    lax.fori_loop(0, SG // 2, two_patches, 0)

    def finish(g, carry):
        post(g, lambda copy: copy.wait())
        return carry

    lax.fori_loop(0, SG, finish, 0)


def make_patches(plan, pf_index, ints, recv, notes, ratio, beams):
    vmem = pl.BlockSpec(memory_space=pltpu.VMEM)
    smem = pl.BlockSpec(memory_space=pltpu.SMEM)
    return pl.pallas_call(
        subgrid_kernel,
        out_shape=(jax.ShapeDtypeStruct((N_SUB, 128, 256), BF16),) * 2,
        in_specs=[smem] * 3 + [vmem] * 9,
        out_specs=(pl.BlockSpec(memory_space=pl.ANY),) * 2,
        scratch_shapes=[
            pltpu.VMEM((SG * 64 + 1, 8, 128), F32),
            pltpu.VMEM((SG * 64 + 8, 128), F32),
            pltpu.VMEM((SG * 64 + 8, 128), F32),
            pltpu.VMEM((2, N_SUB, 128), F32),
            pltpu.SMEM((SG * LIST + SG,), jnp.int32),
            pltpu.VMEM((SG, 512, 128), F32),
            pltpu.VMEM((SG, 128, 256), BF16),
            pltpu.SemaphoreType.DMA((SG,)),
        ],
        compiler_params=pltpu.CompilerParams(vmem_limit_bytes=48 * MIB),
        name="subgrids",
    )(plan, pf_index, ints, recv, notes, ratio, beams, *dft_tables())


HELPERS = 4
RELAYED = 4
TOGETHER = 8
AT_BAD = 8
AT_RELAY = 16
AT_USED = 32
DUMP = 80
AT_ROW = AT_USED + DUMP + 8
AT_COL = AT_ROW + DUMP + 8
PLAN = AT_COL + DUMP + 8
AT_SECOND = N_SUB + HELPERS * RELAYED


def neighbour(tile, k):
    if k < 2:
        return (tile & 28) | ((tile + (1, 3)[k]) & 3)
    return (tile + (4, 28)[k - 2]) & 31


def plan_kernel(me_ref, note_ref, plan_ref, load_scr, mask_scr):
    me = me_ref[0]

    def clear(i, carry):
        for k in range(8):
            plan_ref[i * 8 + k] = 0
        return carry

    def clear_load(i, carry):
        for k in range(8):
            load_scr[i * 8 + k] = 0
        return carry

    lax.fori_loop(0, PLAN // 8, clear, 0)
    lax.fori_loop(0, HELPERS * N_SUB // 8, clear_load, 0)
    for i in range(HELPERS * RELAYED):
        plan_ref[AT_RELAY + i] = -1
    for g in range(SG):
        plan_ref[g] = note_ref[me * 8 + 3, g] >> 1

    def note(entry, used, source, g):
        plan_ref[AT_USED + entry] = used
        plan_ref[AT_ROW + entry] = note_ref[source * 8 + 4, g]
        plan_ref[AT_COL + entry] = note_ref[source * 8 + 5, g] * 128 + note_ref[source * 8 + 6, g]

    def seconds(source):
        mask = jnp.int32(0)
        for g in range(SG):
            mask = mask | (jnp.int32(1) << (note_ref[source * 8 + 3, g] >> 1))
        mask_scr[0] = mask

        def one(g, carry):
            slot = note_ref[source * 8 + 3, g]

            @pl.when((slot & 1) == 1)
            def _():
                tile = slot >> 1
                busy = mask_scr[0]
                best, helper, load = jnp.int32(-1), jnp.int32(0), jnp.int32(RELAYED)
                for k in range(HELPERS):
                    via = neighbour(tile, k)
                    held = load_scr[k * N_SUB + tile]
                    better = (((busy >> via) & 1) == 0) & (held < load)
                    best = jnp.where(better, k, best)
                    helper = jnp.where(better, via, helper)
                    load = jnp.where(better, held, load)

                @pl.when(best >= 0)
                def _():
                    mask_scr[0] = busy | (jnp.int32(1) << helper)
                    load_scr[best * N_SUB + tile] = load + 1
                    place = best * RELAYED + load

                    @pl.when(source == me)
                    def _():
                        plan_ref[g] = helper

                    @pl.when(helper == me)
                    def _():
                        plan_ref[AT_RELAY + place] = source

                    @pl.when(tile == me)
                    def _():
                        note(N_SUB + place, 1, source, g)

                @pl.when(best < 0)
                def _():
                    plan_ref[AT_BAD] = 1

                    @pl.when(source == me)
                    def _():
                        plan_ref[g] = N_SUB + tile

                    @pl.when(tile == me)
                    def _():
                        note(AT_SECOND + source, 1, source, g)

            return carry

        lax.fori_loop(0, SG, one, 0)

    def one_source(source, carry):
        which, any_second = jnp.int32(0), jnp.int32(0)
        for g in range(SG):
            slot = note_ref[source * 8 + 3, g]
            which = jnp.where(slot == 2 * me, g + 1, which)
            any_second = any_second | (slot & 1)
        note(source, jnp.minimum(which, 1), source, jnp.maximum(which - 1, 0))

        @pl.when(any_second > 0)
        def _():
            seconds(source)

        return carry

    lax.fori_loop(0, N_SUB, one_source, 0)


def make_plan(me, ints):
    smem = pl.BlockSpec(memory_space=pltpu.SMEM)
    return pl.pallas_call(
        plan_kernel,
        out_shape=jax.ShapeDtypeStruct((PLAN,), jnp.int32),
        in_specs=[smem] * 2,
        out_specs=smem,
        scratch_shapes=[
            pltpu.SMEM((HELPERS * N_SUB,), jnp.int32),
            pltpu.SMEM((1,), jnp.int32),
        ],
        name="plan",
    )(me, ints)


def relay_kernel(plan_ref, arrived_ref, *outs):
    out_refs, sems = outs[:HELPERS], outs[HELPERS]

    def each(act):
        for k in range(HELPERS):
            for c in range(RELAYED):
                source = plan_ref[AT_RELAY + k * RELAYED + c]

                @pl.when(source >= 0)
                def _(k=k, c=c, source=source):
                    act(
                        pltpu.make_async_copy(
                            arrived_ref.at[source], out_refs[k].at[c], sems.at[k * RELAYED + c]
                        )
                    )

    each(lambda copy: copy.start())
    each(lambda copy: copy.wait())


def relay(plan, arrived):
    hbm = pl.BlockSpec(memory_space=pl.ANY)
    return pl.pallas_call(
        relay_kernel,
        out_shape=(jax.ShapeDtypeStruct((RELAYED, 128, 256), BF16),) * HELPERS,
        in_specs=[pl.BlockSpec(memory_space=pltpu.SMEM), hbm],
        out_specs=(hbm,) * HELPERS,
        scratch_shapes=[pltpu.SemaphoreType.DMA((HELPERS * RELAYED,))],
        name="relay",
    )(plan, arrived)


def deposit_kernel(firsts, plan_ref, *refs):
    recv_refs, out_ref, list_scr = refs[:-2], refs[-2], refs[-1]
    out_ref[...] = jnp.zeros_like(out_ref)
    tall = SUBPIX + 8
    lane = lax.broadcasted_iota(jnp.int32, (2 * tall, 256), 1)
    blank = jnp.zeros((8, 256), F32)

    def placed(entry, recv_ref, slot, real):
        row = jnp.where(real, plan_ref[AT_ROW + entry], 0)
        col = jnp.where(real, plan_ref[AT_COL + entry], 0)
        top = pl.multiple_of(jnp.minimum((row // 8) * 8, BAND - tall), 8)
        start = pl.multiple_of(jnp.minimum((col // 128) * 128, TILE - 256), 128)
        shift = col - start
        patch = recv_ref[slot].astype(F32)
        patch = jnp.concatenate([patch[:SUBPIX], blank, patch[SUBPIX:], blank], 0)
        patch = pltpu.roll(patch, row - top, 0)
        inside = (lane >= shift) & (lane < jnp.where(real, shift + SUBPIX, shift))
        even = pltpu.roll(patch, shift, 1)
        odd = pltpu.roll(patch, lax.rem(shift + 192, 256), 1)
        parts = []
        for q in range(4):
            moved = (even, odd)[q & 1]
            if q >= 2:
                moved = jnp.concatenate([moved[:, 128:], moved[:, :128]], 1)
            parts.append(jnp.where(inside, moved, 0.0))
        return parts, top, start

    def add(parts, top, start):
        for q in range(4):
            for s in range(2):
                spot = (0, 2 * q + s, pl.ds(top, tall), pl.ds(start, 256))
                out_ref[spot] += parts[q][s * tall : (s + 1) * tall]

    def add_listed(first, recv_ref):
        def collect(slot, count):
            list_scr[count] = slot
            return count + plan_ref[AT_USED + first + slot]

        count = lax.fori_loop(0, N_SUB, collect, jnp.int32(0))
        for k in range(TOGETHER):
            list_scr[count + k] = 0

        def some(step, carry):
            ready = []
            for k in range(TOGETHER):
                at = step * TOGETHER + k
                slot = list_scr[at]
                ready.append(placed(first + slot, recv_ref, slot, at < count))
            for one in ready:
                add(*one)
            return carry

        lax.fori_loop(0, (count + TOGETHER - 1) // TOGETHER, some, 0)

    add_listed(firsts[0], recv_refs[0])

    def relayed(slot, carry):
        reals = [plan_ref[AT_USED + first + slot] for first in firsts[1 : 1 + HELPERS]]

        @pl.when(sum(reals) > 0)
        def _():
            ready = [
                placed(first + slot, recv_ref, slot, real > 0)
                for first, recv_ref, real in zip(firsts[1:], recv_refs[1:], reals)
            ]
            for one in ready:
                add(*one)

        return carry

    lax.fori_loop(0, RELAYED, relayed, 0)
    for first, recv_ref in zip(firsts[1 + HELPERS :], recv_refs[1 + HELPERS :]):
        add_listed(first, recv_ref)


def deposit(plan, firsts, patches):
    vmem = pl.BlockSpec(memory_space=pltpu.VMEM)
    smem = pl.BlockSpec(memory_space=pltpu.SMEM)
    return pl.pallas_call(
        functools.partial(deposit_kernel, firsts),
        out_shape=jax.ShapeDtypeStruct((1, 8, BAND, TILE), F32),
        in_specs=[smem] + [vmem] * len(patches),
        out_specs=vmem,
        scratch_shapes=[pltpu.SMEM((N_SUB + TOGETHER,), jnp.int32)],
        compiler_params=pltpu.CompilerParams(vmem_limit_bytes=48 * MIB),
        name="deposit",
    )(plan, *patches)


def shards(
    visibilities,
    row_positions,
    channel_ratio,
    row_subgrid,
    row_count,
    beam_terms,
    subgrid_tile,
    offset_rows,
    offset_cols,
):
    me_sub = lax.axis_index("sub")
    me_pf = lax.axis_index("pf")
    scalars = jnp.concatenate([subgrid_tile[:, 0], offset_rows, offset_cols, row_count])
    send = dispatch(
        scalars, visibilities, row_positions, row_subgrid.reshape(ROWS // 128, 128)
    )
    first = lax.all_to_all(send, "sub", split_axis=0, concat_axis=0, tiled=True)
    recv = jnp.transpose(first[:, :64].reshape(N_SUB, N_PF, 8, 128), (1, 0, 2, 3))
    recv = recv.reshape(N_PF, N_SUB * 8, 128)
    recv = lax.all_to_all(recv, "pf", split_axis=0, concat_axis=0, tiled=True)

    ratio = jnp.repeat(channel_ratio.reshape(8, 8).T.reshape(64), 2)[None, :]
    ints = first[:, 64:72].astype(jnp.int32).reshape(N_SUB * 8, 128)
    plan = make_plan(me_sub.reshape(1), ints)
    bad = plan[AT_BAD] > 0
    patches, second = make_patches(
        plan, me_pf.reshape(1), ints, recv, first, ratio,
        beam_terms.reshape(SG, 2, 8, SUBPIX, SUBPIX),
    )
    arrived = lax.all_to_all(patches, "sub", split_axis=0, concat_axis=0, tiled=True)
    relayed = [
        lax.ppermute(block, "sub", [(neighbour(t, k), t) for t in range(N_SUB)])
        for k, block in enumerate(relay(plan, arrived))
    ]
    firsts = (0,) + tuple(N_SUB + k * RELAYED for k in range(HELPERS))

    def with_second(plan, second, *blocks):
        late = lax.all_to_all(second, "sub", split_axis=0, concat_axis=0, tiled=True)
        return deposit(plan, firsts + (AT_SECOND,), blocks + (late,))

    def without(plan, second, *blocks):
        return deposit(plan, firsts, blocks)

    return lax.cond(bad, with_second, without, plan, second, arrived, *relayed)


def solution(mesh):
    in_specs = (
        P(None, "pf", "sub"),
        P(None, "sub"),
        P(),
        P("sub", None),
        P("sub"),
        P(("sub", "pf"), None, None, None),
        P(("sub", "pf"), None),
        P(("sub", "pf")),
        P(("sub", "pf")),
    )
    out_specs = P(("sub", "pf"), None, None, None)
    return jax.shard_map(shards, mesh=mesh, in_specs=in_specs, out_specs=out_specs, check_vma=False)
```
